128 devices in a mesh: store: 4 (over z), ctx: 16 (over y, x), head: 2 (over core).
Axes of the slice: x: 4, y: 4, z: 4, core: 2. Of those that a mesh axis runs over, the one named last changes fastest.
Arguments:
- queries: bfloat16 [512, 64, 128], P(('store', 'ctx', 'head')), may hold values from -12 to 12
- suffix_k: bfloat16 [512, 8, 128], P(('store', 'ctx'), 'head'), may hold values from -6 to 6
- suffix_v: bfloat16 [512, 8, 128], P(('store', 'ctx'), 'head'), may hold values from -6 to 6
- pool_k: bfloat16 [1024, 256, 8, 128], P(('store', 'ctx'), None, 'head'), may hold values from -6 to 6
- pool_v: bfloat16 [1024, 256, 8, 128], P(('store', 'ctx'), None, 'head'), may hold values from -6 to 6
- list_holder: int32 [512, 1], P(('store', 'ctx')), may hold values from 0 to 3; in each aligned block of 8 rows (0 to 7, 8 to 15, ...) at most 3 rows name the same one
- list_slot: int32 [512], P(('store', 'ctx')), may hold values from 0 to 15
- list_valid: int32 [512], P(('store', 'ctx')), may hold values from 0 to 256, as said below
Outputs:
- mixed: bfloat16 [512, 64, 128], P(('store', 'ctx', 'head'))
The draws below stay inside these ranges and needn't reach their ends.
Inputs may be any that keep to these rules, and one draw needn't show every extreme that they name: `list_holder`: at most 3 of the 8 entries of one index of store+ctx name the same store index. `list_valid`: 0 marks a padding entry; each index of store+ctx has at least one full block among its 8 entries.
All inputs are finite; a program needn't handle non-finite values.
Results may differ from the reference program's by a relative error of at most 0.0016.
Values may be sent and summed in bfloat16 or wider, within the bound.
A program may use at most 128 MiB of HBM per device.

```python
import math
import jax
import jax.numpy as jnp
import numpy as np
from jax import lax

QH = 64
KVH = 8
HD = 128
BLOCK = 256
SUF_DEV = 4
LIST_DEV = 8
SLOTS = 16
WORKERS = 64
LISTS = 512
POOL = 1024
SUF = 512
MOST = 3
N_STORE = 4
N_CTX = 16
N_HEAD = 2


def draw_queries(key, part):
    key = jax.random.fold_in(key, 5)
    key_one = jax.random.fold_in(key, 0)
    values = jnp.clip(3.0 * jax.random.normal(key_one, (SUF, QH, HD), jnp.float32), -12.0, 12.0)
    return values.astype(jnp.bfloat16)


def draw_pool_k(key, part):
    key = jax.random.fold_in(key, 7)
    key_one = jax.random.fold_in(key, 0)
    shape = (POOL, BLOCK, KVH, HD)
    values = jnp.clip(jax.random.normal(key_one, shape, jnp.float32), -6.0, 6.0)
    return values.astype(jnp.bfloat16)


def draw_list_valid(key, part):
    key = jax.random.fold_in(key, 11)
    key_one, key_two, key_three = jax.random.split(key, 3)
    counts = jax.random.randint(key_one, (WORKERS, LIST_DEV), 1, BLOCK + 1)
    padding = jax.random.randint(key_two, (WORKERS, LIST_DEV), 0, 4) == 0
    counts = jnp.where(padding, 0, counts)
    full_at = jax.random.randint(key_three, (WORKERS, 1), 0, LIST_DEV)
    counts = jnp.where(jnp.arange(LIST_DEV)[None, :] == full_at, BLOCK, counts)
    return counts.reshape(WORKERS * LIST_DEV).astype(jnp.int32)


def set_ends(values, rng, low, largest):
    longest = values.shape.index(max(values.shape))
    spots = []
    for shift in (0, 1):
        where = [jax.random.randint(jax.random.fold_in(rng, axis), (), 0, length) for axis, length in enumerate(values.shape)]
        where[longest] = (where[longest] + shift) % values.shape[longest]
        spots.append(tuple(where))
    return values.at[spots[0]].set(low).at[spots[1]].set(largest)


def shard_levels(key, dims, cuts, smallest, high):
    gain, own = 1.0, jax.random.fold_in(key, 6)
    for dim, blocks in cuts:
        draws = jnp.exp(jax.random.uniform(jax.random.fold_in(own, dim), (blocks,), jnp.float32, smallest / len(cuts), high / len(cuts)))
        gain = gain * jnp.repeat(draws, dims[dim] // blocks).reshape([-1 if axis == dim else 1 for axis in range(len(dims))])
    return gain


def routed_block(rng, own, number, rows, amount, top, reach, skew):
    sequence = jax.random.permutation(rng, amount)
    heavy_load, ordinary = shares(amount, rows * top, reach, skew, True), shares(amount, rows * top, reach, skew, False)
    places = jnp.arange(amount)

    def named(lengths, rotation):
        used = int((lengths > 0).sum())
        fixed = max(1, used // 4)
        moved = fixed + (places - fixed + rotation * (used - fixed)) % max(1, amount - fixed)
        return jnp.zeros((amount,), jnp.int32).at[sequence[jnp.where(places < fixed, places, moved)]].set(jnp.asarray(lengths, jnp.int32))

    lengths = jnp.where(number % 4 == 0, named(heavy_load, number // 4), named(ordinary, number - number // 4 - 1))
    mixed = jax.random.permutation(jax.random.fold_in(own, 3), amount)
    giver, receiver = mixed[0:amount // 2 * 2:2], mixed[1:amount // 2 * 2:2]
    margin = jnp.minimum(lengths[giver] - 1, reach - lengths[receiver]) // 2
    margin = jnp.where((giver == sequence[0]) | (receiver == sequence[0]) | (lengths[receiver] == 0), 0, jnp.maximum(margin, 0))
    moved = jax.random.randint(jax.random.fold_in(own, 4), (amount // 2,), 0, 1 << 20) % (margin + 1)
    lengths = lengths.at[giver].add(-moved).at[receiver].add(moved)
    labels = jnp.searchsorted(jnp.cumsum(lengths), jnp.arange(rows * top), side="right").astype(jnp.int32)
    table = labels.reshape(top, rows).T
    table = table[jax.random.permutation(jax.random.fold_in(own, 1), rows)]
    rotation = jax.random.randint(jax.random.fold_in(own, 2), (rows, 1), 0, top)
    return jnp.take_along_axis(table, (jnp.arange(top)[None, :] + rotation) % top, axis=1)


def shares(count, total, limit, skew, full):
    weights = [(1 << 20) // math.isqrt(grade ** skew) + 1 for grade in range(1, count + 1)]
    largest = limit if full else min(limit, max(-(-total // count), total * weights[0] // sum(weights)))
    least = 1 if total - largest >= count - 1 else 0
    given, spare = [largest] + [least] * (count - 1), total - largest - least * (count - 1)
    while spare > 0:
        movable = [i for i in range(1, count) if given[i] < largest] or [i for i in range(1, count) if given[i] < limit]
        mass, budget = sum([weights[i] for i in movable]), spare
        for i in movable:
            extra = min(limit - given[i], max(1, budget * weights[i] // mass), spare)
            given[i] = given[i] + extra
            spare = spare - extra
    return np.array(given)


def gaussian(stream_key, extent, width, limit, shards=(), kind=jnp.bfloat16):
    loudness = shard_levels(stream_key, extent, shards, -0.22, 0.18) if shards else 1.0
    values = jax.random.normal(stream_key, extent, jnp.float32) * width * loudness
    return jnp.minimum(jnp.maximum(values, -limit), limit).astype(kind)


def setup_inputs(seed: int = 0) -> dict:
    key_list = jax.random.split(jax.random.key(seed), 9)
    queries = draw_queries(jax.random.fold_in(key_list[8], 71), 0)
    suffix_k = gaussian(key_list[1], (SUF, KVH, HD), 1.4, 6.0, ((0, 64), (1, 2)))
    suffix_v = gaussian(key_list[2], (SUF, KVH, HD), 1.0, 6.0, ((0, 64), (1, 2)))
    pool_k = draw_pool_k(jax.random.fold_in(key_list[8], 71), 0)
    pool_v = gaussian(key_list[4], (POOL, BLOCK, KVH, HD), 1.0, 6.0, ((0, 64), (2, 2)))
    list_holder_keys = jax.random.split(jax.random.fold_in(key_list[5], 1), LISTS // LIST_DEV)
    list_holder_turns = jax.random.permutation(jax.random.fold_in(key_list[5], 3), LISTS // LIST_DEV)
    list_holder = jax.vmap(lambda own, number: routed_block(jax.random.fold_in(key_list[5], 2), own, number, LIST_DEV, N_STORE, 1, MOST, 2))(list_holder_keys, list_holder_turns).reshape((LISTS, 1))
    list_slot = set_ends(jax.random.randint(key_list[6], (LISTS,), 0, SLOTS), jax.random.fold_in(key_list[6], 1), 0, SLOTS - 1).astype(jnp.int32)
    list_valid = draw_list_valid(jax.random.fold_in(key_list[8], 71), 0)
    return dict(queries=queries, suffix_k=suffix_k, suffix_v=suffix_v, pool_k=pool_k, pool_v=pool_v, list_holder=list_holder, list_slot=list_slot, list_valid=list_valid)


NEG_FILL = -1e+30

def block_terms(query_all, key_tile, value_tile, live_mask):
    query_rows, head_count, head_width = query_all.shape
    kv_count = key_tile.shape[1]
    grouped = query_all.astype(jnp.float32).reshape(query_rows, kv_count, head_count // kv_count, head_width)
    scores = jnp.einsum('rgqd,kgd->rgqk', grouped, key_tile.astype(jnp.float32)) / math.sqrt(head_width)
    live_wide = live_mask[:, None, None, :]
    masked = jnp.where(live_wide, scores, NEG_FILL)
    block_peak = lax.optimization_barrier(jnp.max(masked, axis=3))
    weights = jnp.where(live_wide, jnp.exp(masked - block_peak[..., None]), 0.0).astype(jnp.bfloat16)
    weights_wide = weights.astype(jnp.float32)
    total_sum = lax.optimization_barrier(jnp.sum(weights_wide, axis=3))
    weighted = jnp.einsum('rgqk,kgd->rgqd', weights_wide, value_tile.astype(jnp.float32))
    return (block_peak.reshape(query_rows, head_count), total_sum.reshape(query_rows, head_count), weighted.reshape(query_rows, head_count, head_width))

def merge_terms(carried, incoming):
    peak_old, total_old, weighted_old = carried
    peak_new, total_new, weighted_new = incoming
    joined = jnp.maximum(peak_old, peak_new)
    factor_old = jnp.exp(peak_old - joined)
    factor_new = jnp.exp(peak_new - joined)
    return (joined, total_old * factor_old + total_new * factor_new, weighted_old * factor_old[..., None] + weighted_new * factor_new[..., None])

def reference(queries, suffix_k, suffix_v, pool_k, pool_v, list_holder, list_slot, list_valid):
    entries = jnp.arange(LISTS, dtype=jnp.int32)
    column = entries // LIST_DEV % N_CTX
    slot_index = ((list_holder[:, 0] * N_CTX + column) * SLOTS + list_slot).astype(jnp.int32)
    positions = jnp.arange(BLOCK, dtype=jnp.int32)
    start_state = (jnp.full((SUF, QH), NEG_FILL, jnp.float32), jnp.zeros((SUF, QH), jnp.float32), jnp.zeros((SUF, QH, HD), jnp.float32))

    def prefix_step(carried, element):
        slot_at, valid_count = element
        key_tile = lax.dynamic_index_in_dim(pool_k, slot_at, 0, keepdims=False)
        value_tile = lax.dynamic_index_in_dim(pool_v, slot_at, 0, keepdims=False)
        live_mask = jnp.broadcast_to(positions[None, :] < valid_count, (SUF, BLOCK))
        return (merge_terms(carried, block_terms(queries, key_tile, value_tile, live_mask)), None)
    carried, _unused = lax.scan(prefix_step, start_state, (slot_index, list_valid))
    group_size = SUF_DEV * N_HEAD
    query_index = jnp.arange(SUF, dtype=jnp.int32)
    offsets = (jnp.arange(WORKERS, dtype=jnp.int32) * group_size).astype(jnp.int32)

    def suffix_step(carried, offset):
        key_tile = lax.dynamic_slice_in_dim(suffix_k, offset, group_size, 0)
        value_tile = lax.dynamic_slice_in_dim(suffix_v, offset, group_size, 0)
        key_index = offset + jnp.arange(group_size, dtype=jnp.int32)
        live_mask = key_index[None, :] <= query_index[:, None]
        return (merge_terms(carried, block_terms(queries, key_tile, value_tile, live_mask)), None)
    carried, _unused = lax.scan(suffix_step, carried, offsets)
    final_peak, total_sum, weighted = carried
    return (weighted / total_sum[..., None]).astype(jnp.bfloat16)
```

```python
import functools
import math

import jax
import jax.numpy as jnp
from jax import lax
from jax.experimental import pallas as pl
from jax.experimental.pallas import tpu as pltpu
from jax.sharding import PartitionSpec as P

NEG = -1e30
EXP2_SCALE = math.log2(math.e) / math.sqrt(128)
NT = (((1,), (1,)), ((), ()))
NN = (((1,), (0,)), ((), ()))
MESH = pl.DeviceIdType.MESH
PARTS = ((0, 80), (80, 80), (160, 96))
JOBS = 12
TOP16 = 32767.0


def matmul(a, b, dims=NN):
    return lax.dot_general(a, b, dims, preferred_element_type=jnp.float32)


def position():
    ctx = lax.axis_index("ctx")
    return [lax.axis_index("store"), ctx // 4, ctx % 4], lax.axis_index("head")


def device(place, core):
    return (place[0], place[1] * 4 + place[2], core)


def along(place, axis, step):
    moved = list(place)
    moved[axis] = (place[axis] + step) % 4
    return moved


def greet(place, core):
    barrier = pltpu.get_barrier_semaphore()
    for axis in range(3):
        for step in (1, 2, 3):
            pl.semaphore_signal(barrier, 1, device_id=device(along(place, axis, step), core), device_id_type=MESH)
    pl.semaphore_signal(barrier, 1, device_id=device(place, 1 - core), device_id_type=MESH)
    pl.semaphore_wait(barrier, 10)


def gather_kernel(q_ref, list_ref, all_ref, lists_ref, mine, theirs, send, own, swap_sem, list_sem, own_sem, send_sem, recv_sem):
    place, core = position()
    greet(place, core)
    swap = pltpu.make_async_remote_copy(
        q_ref.at[:, pl.ds((1 - core) * 32, 32), :], theirs, swap_sem.at[0], swap_sem.at[1],
        device_id=device(place, 1 - core), device_id_type=MESH)
    swap.start()
    lists = []
    for step in (1, 2, 3):
        copy = pltpu.make_async_remote_copy(
            list_ref, lists_ref.at[place[0]], list_sem.at[0, step - 1], list_sem.at[1, step - 1],
            device_id=device(along(place, 0, step), core), device_id_type=MESH)
        copy.start()
        lists.append(copy)
    own_lists = pltpu.make_async_copy(list_ref, lists_ref.at[place[0]], own_sem.at[1])
    own_lists.start()

    def grouped(tokens):
        wide = tokens.astype(jnp.float32).reshape(4, 4, 8, 128)
        return jnp.stack([wide[:, g].reshape(32, 128) for g in range(4)]).astype(jnp.bfloat16)

    mine[...] = q_ref[:, pl.ds(core * 32, 32), :]
    send[:, pl.ds(core * 32, 32), :] = grouped(mine[...])
    swap.wait()
    send[:, pl.ds((1 - core) * 32, 32), :] = grouped(theirs[...])
    own[...] = send[...].reshape(256, 128)
    keep = pltpu.make_async_copy(own, all_ref.at[place[0], place[1], place[2]], own_sem.at[0])
    keep.start()

    def copies(part, phase):
        order = [(part + i) % 3 for i in range(3)]
        rows = pl.ds(*PARTS[part])
        where = [slice(None) if axis in order[:phase] else place[axis] for axis in range(3)]
        block = all_ref.at[where[0], where[1], where[2], rows]
        source = own.at[rows] if phase == 0 else block
        return [
            pltpu.make_async_remote_copy(
                source, block, send_sem.at[part, phase, step - 1], recv_sem.at[part, phase, step - 1],
                device_id=device(along(place, order[phase], step), core), device_id_type=MESH)
            for step in (1, 2, 3)
        ]

    started = []
    for phase in range(3):
        for part in range(3):
            if phase:
                for copy in started[(phase - 1) * 3 + part]:
                    copy.wait_recv()
            elif part == 0:
                pass
            if phase == 1 and part == 0:
                keep.wait()
            now = copies(part, phase)
            for copy in now:
                copy.start()
            started.append(now)
    for part in range(3):
        for copy in started[6 + part]:
            copy.wait_recv()
    for group in started:
        for copy in group:
            copy.wait_send()
    for copy in lists:
        copy.wait()
    own_lists.wait()


def gather_queries(queries, lists):
    hbm = pl.BlockSpec(memory_space=pl.ANY)
    vmem = pl.BlockSpec(memory_space=pltpu.VMEM)
    dma = pltpu.SemaphoreType.DMA
    return pl.pallas_call(
        gather_kernel,
        out_shape=[jax.ShapeDtypeStruct((4, 4, 4, 256, 128), jnp.bfloat16), jax.ShapeDtypeStruct((4, 8, 128), jnp.int32)],
        in_specs=[vmem, vmem],
        out_specs=[hbm, hbm],
        scratch_shapes=[
            pltpu.VMEM((4, 32, 128), jnp.bfloat16), pltpu.VMEM((4, 32, 128), jnp.bfloat16),
            pltpu.VMEM((4, 64, 128), jnp.bfloat16), pltpu.VMEM((256, 128), jnp.bfloat16),
            dma((2,)), dma((2, 3)), dma((2,)), dma((3, 3, 3)), dma((3, 3, 3)),
        ],
        compiler_params=pltpu.CompilerParams(collective_id=0, has_side_effects=True, vmem_limit_bytes=16 * 2**20),
        name="gather_queries",
    )(queries, lists)


def attend_kernel(list_ref, q_ref, pk_ref, pv_ref, sk_ref, sv_ref, o_ref, side_ref,
                  kj, vj, peak, acc, jobs, count, sem):
    @pl.when(pl.program_id(0) == 0)
    def prepare():
        store = lax.axis_index("store")
        count[0] = 0

        def look(i, _):
            row, e = i // 8, i % 8
            slot, valid = list_ref[row, 1, e], list_ref[row, 2, e]

            @pl.when((list_ref[row, 0, e] == store) & (valid > 0))
            def _():
                n = count[0]
                jobs[0, n] = slot
                jobs[1, n] = valid
                count[0] = n + 1
                pltpu.make_async_copy(pk_ref.at[slot], kj.at[n], sem.at[0, n]).start()
                pltpu.make_async_copy(pv_ref.at[slot], vj.at[n, :, 0:128], sem.at[1, n]).start()
            return 0

        lax.fori_loop(0, 32, look, 0)

        def fix(n, _):
            slot, valid = jobs[0, n], jobs[1, n]
            pltpu.make_async_copy(pk_ref.at[slot], kj.at[n], sem.at[0, n]).wait()
            pltpu.make_async_copy(pv_ref.at[slot], vj.at[n, :, 0:128], sem.at[1, n]).wait()
            live_row = lax.broadcasted_iota(jnp.int32, (256, 128), 0) < valid
            live_lane = lax.broadcasted_iota(jnp.int32, (128, 256), 1) < valid
            for g in range(4):
                keys = kj[n, g].astype(jnp.float32)
                kj[n, g] = jnp.where(live_row, keys, keys[0:1]).astype(jnp.bfloat16)
                vj[n, g, 0:128] = jnp.where(live_lane, vj[n, g, 0:128].astype(jnp.float32), 0.0).astype(jnp.bfloat16)
                vj[n, g, 128:144] = live_lane[0:16].astype(jnp.float32).astype(jnp.bfloat16)
            return 0

        lax.fori_loop(0, count[0], fix, 0)

    pair = pl.program_id(0)
    suffix_at = (lax.axis_index("store") * 16 + lax.axis_index("ctx")) * 8
    key_at = suffix_at + lax.broadcasted_iota(jnp.int32, (8, 4096), 0)
    query_at = lax.broadcasted_iota(jnp.int32, (8, 4096), 1) // 8
    live = key_at <= query_at
    for half in range(2):
        q = q_ref[:, half * 64:(half + 1) * 64, :].reshape(4096, 128)
        s = matmul(sk_ref[pair * 2 + half], q, NT)[0:8]
        s = jnp.where(live, s, NEG)
        t = jnp.max(s, axis=0, keepdims=True)
        w = jnp.where(live, jnp.exp2((s - t) * EXP2_SCALE), 0.0)
        w = jnp.concatenate([w, jnp.zeros((120, 4096), jnp.float32)], axis=0).astype(jnp.bfloat16)
        acc[half] = matmul(sv_ref[pair * 2 + half], w)
        peak[half] = t

        def block(n, _):
            s = matmul(kj[n, pair * 2 + half], q, NT)
            t = jnp.max(s, axis=0, keepdims=True)
            w = jnp.exp2((s - t) * EXP2_SCALE).astype(jnp.bfloat16)
            x = matmul(vj[n, pair * 2 + half], w)
            m = peak[half]
            top = jnp.maximum(m, t)
            acc[half] = acc[half] * jnp.exp2((m - top) * EXP2_SCALE) + x * jnp.exp2((t - top) * EXP2_SCALE)
            peak[half] = top
            return 0

        lax.fori_loop(0, count[0], block, 0)

    low = lax.broadcasted_iota(jnp.int32, (1, 128), 1) < 64

    def emit(i, _):
        lanes = pl.ds(pl.multiple_of(i * 128, 128), 128)
        a, b = acc[0, 0:136, lanes], acc[1, 0:136, lanes]
        pa, pb = peak[0, :, lanes], peak[1, :, lanes]
        for odd in range(2):
            if odd:
                whole = jnp.where(low, pltpu.roll(a, 64, 1), b)
                top = jnp.where(low, pltpu.roll(jnp.broadcast_to(pa, (8, 128)), 64, 1)[0:1], pb)
            else:
                whole = jnp.where(low, a, pltpu.roll(b, 64, 1))
                top = jnp.where(low, pa, pltpu.roll(jnp.broadcast_to(pb, (8, 128)), 64, 1)[0:1])
            values, scale = encode(whole[0:128])
            o_ref[i * 2 + odd, 0] = values
            side_ref[i * 2 + odd, 0] = jnp.concatenate([top, whole[128:129], scale, jnp.zeros((5, 128), jnp.float32)], axis=0)
        return 0

    lax.fori_loop(0, 32, emit, 0)


def encode(x):
    largest = jnp.maximum(jnp.max(jnp.abs(x), axis=0, keepdims=True), 1e-30)
    whole = jnp.round(x * (TOP16 / largest)).astype(jnp.int32).astype(jnp.int16)
    return whole, largest * (1.0 / TOP16)


def attend(lists, gathered, pool_k, pool_v, suffix_k, suffix_v):
    hbm = pl.BlockSpec(memory_space=pl.ANY)
    return pl.pallas_call(
        attend_kernel,
        grid=(2,),
        in_specs=[
            pl.BlockSpec(memory_space=pltpu.SMEM),
            pl.BlockSpec((64, 128, 128), lambda i: (0, i, 0)),
            hbm, hbm,
            pl.BlockSpec((4, 16, 128), lambda i: (0, 0, 0)),
            pl.BlockSpec((4, 144, 128), lambda i: (0, 0, 0)),
        ],
        out_specs=[pl.BlockSpec((64, 1, 128, 128), lambda i: (0, i, 0, 0)), pl.BlockSpec((64, 1, 8, 128), lambda i: (0, i, 0, 0))],
        out_shape=[jax.ShapeDtypeStruct((64, 2, 128, 128), jnp.int16), jax.ShapeDtypeStruct((64, 2, 8, 128), jnp.float32)],
        scratch_shapes=[
            pltpu.VMEM((JOBS, 4, 256, 128), jnp.bfloat16), pltpu.VMEM((JOBS, 4, 144, 256), jnp.bfloat16),
            pltpu.VMEM((2, 1, 4096), jnp.float32), pltpu.VMEM((2, 144, 4096), jnp.float32),
            pltpu.SMEM((2, JOBS), jnp.int32), pltpu.SMEM((1,), jnp.int32), pltpu.SemaphoreType.DMA((2, JOBS)),
        ],
        compiler_params=pltpu.CompilerParams(vmem_limit_bytes=60 * 2**20),
        name="attend",
    )(lists, gathered, pool_k, pool_v, suffix_k, suffix_v)


def merge(parts):
    top = functools.reduce(jnp.maximum, [side[0:1] for _, side in parts])
    total, weighted = 0.0, 0.0
    for values, side in parts:
        factor = jnp.exp2((side[0:1] - top) * EXP2_SCALE)
        total = total + side[1:2] * factor
        weighted = weighted + values.astype(jnp.int32).astype(jnp.float32) * (side[2:3] * factor)
    return weighted, top, total


def merge_kernel(o_ref, side_ref, out_ref, r1, r1s, p1, p1s, r2, r2s, p2, p2s, r3, r3s, rows, swapped, wide,
                 send1, recv1, send2, recv2, send3, recv3, swap_sem):
    place, core = position()
    greet(place, core)

    def least(color, a, u):
        return (color - a - u + 9) % 3

    def number(color, a, u, v):
        at = [None] * 3
        for axis, value in zip([(color + i) % 3 for i in range(3)], (a, u, v)):
            at[axis] = value
        return at[0] * 16 + at[1] * 4 + at[2]

    def two(source, source_side, target, target_side, send, recv, to):
        return [
            pltpu.make_async_remote_copy(source, target, send.at[0], recv.at[0], device_id=to, device_id_type=MESH),
            pltpu.make_async_remote_copy(source_side, target_side, send.at[1], recv.at[1], device_id=to, device_id_type=MESH),
        ]

    def first(color, step, w):
        a = (place[color] + step) % 4
        u = w // 2
        v = least(color, a, u) + 3 * (w % 2)
        chunk = jnp.minimum(number(color, a, u, v), 63)
        return v <= 3, two(
            o_ref.at[chunk], side_ref.at[chunk], r1.at[color, step - 1, w], r1s.at[color, step - 1, w],
            send1.at[color, step - 1, w], recv1.at[color, step - 1, w], device(along(place, color, step), core))

    def each(function):
        for color in range(3):
            for step in (2, 1, 3):
                def go(w, _):
                    there, copies = first(color, step, w)

                    @pl.when(there)
                    def _():
                        for copy in copies:
                            function(copy)
                    return 0
                lax.fori_loop(0, 8, go, 0)

    each(lambda copy: copy.start())

    def second(color, u, half):
        axis = (color + 1) % 3
        step = (u - place[axis] + 4) % 4
        to = list(place)
        to[axis] = u
        at = jnp.maximum(step - 1, 0)
        return two(p1.at[color, u * 2 + half], p1s.at[color, u * 2 + half], r2.at[color, at, half], r2s.at[color, at, half],
                   send2.at[color, at, half], recv2.at[color, at, half], device(to, core))

    def fold(sources, target, target_side):
        for pair in range(2):
            weighted, top, total = merge([(values[pair], side[pair]) for values, side in sources])
            values, scale = encode(weighted)
            target[pair] = values
            target_side[pair] = jnp.concatenate([top, total, scale, jnp.zeros((5, 128), jnp.float32)], axis=0)

    for color in range(3):
        a = place[color]
        second_at = place[(color + 1) % 3]

        def go(w, _):
            u = w // 2
            v = least(color, a, u) + 3 * (w % 2)

            @pl.when(v <= 3)
            def _():
                for step in (1, 2, 3):
                    for copy in first(color, step, w)[1]:
                        copy.wait_recv()
                chunk = jnp.minimum(number(color, a, u, v), 63)
                fold([(o_ref.at[chunk], side_ref.at[chunk])]
                     + [(r1.at[color, k, w], r1s.at[color, k, w]) for k in range(3)],
                     p1.at[color, w], p1s.at[color, w])

                @pl.when(u != second_at)
                def _():
                    for copy in second(color, u, w % 2):
                        copy.start()
            return 0

        lax.fori_loop(0, 8, go, 0)

    def third(color, half, v):
        axis = (color + 2) % 3
        at = jnp.maximum((v - place[axis] + 4) % 4 - 1, 0)
        to = list(place)
        to[axis] = v
        return two(p2.at[color, half], p2s.at[color, half], r3.at[at], r3s.at[at],
                   send3.at[color, at], recv3.at[at], device(to, core))

    for color in range(3):
        a, b, c = place[color], place[(color + 1) % 3], place[(color + 2) % 3]
        for half in range(2):
            v = least(color, a, b) + 3 * half

            @pl.when(v <= 3)
            def _():
                for k in range(3):
                    for copy in two(p1.at[color, 0], p1s.at[color, 0], r2.at[color, k, half], r2s.at[color, k, half],
                                    send2.at[color, k, half], recv2.at[color, k, half], device(along(place, (color + 1) % 3, 1), core)):
                        copy.wait_recv()
                slot = b * 2 + half
                fold([(p1.at[color, slot], p1s.at[color, slot])]
                     + [(r2.at[color, k, half], r2s.at[color, k, half]) for k in range(3)],
                     p2.at[color, half], p2s.at[color, half])

                @pl.when(v != c)
                def _():
                    for copy in third(color, half, v):
                        copy.start()

    color = (place[0] + place[1] + place[2]) % 3
    for k in range(3):
        for copy in two(p2.at[0, 0], p2s.at[0, 0], r3.at[k], r3s.at[k], send3.at[0, k], recv3.at[k],
                        device(along(place, 0, 1), core)):
            copy.wait_recv()
    third_at = jnp.where(color == 0, place[2], jnp.where(color == 1, place[0], place[1]))
    half = third_at // 3
    mine = [(p2.at[color, half], p2s.at[color, half])] + [(r3.at[k], r3s.at[k]) for k in range(3)]
    for pair in range(2):
        weighted, top, total = merge([(values[pair], side[pair]) for values, side in mine])
        done = jnp.transpose(weighted / total)
        for g in range(2):
            for owner in range(2):
                rows[owner, pair * 2 + g] = done[g * 64 + owner * 32:g * 64 + (owner + 1) * 32]
    swap = pltpu.make_async_remote_copy(rows.at[1 - core], swapped, swap_sem.at[0], swap_sem.at[1],
                                        device_id=device(place, 1 - core), device_id_type=MESH)
    swap.start()

    def tokens(grouped):
        split = grouped.reshape(4, 4, 8, 128)
        return jnp.stack([jnp.concatenate([split[g, t] for g in range(4)], axis=0) for t in range(4)])

    wide[:, pl.ds(pl.multiple_of(core * 32, 32), 32), :] = tokens(rows[core])
    swap.wait()
    wide[:, pl.ds(pl.multiple_of((1 - core) * 32, 32), 32), :] = tokens(swapped[...])
    out_ref[...] = wide[...].astype(jnp.bfloat16)

    each(lambda copy: copy.wait_send())
    for color in range(3):
        a, b, c = place[color], place[(color + 1) % 3], place[(color + 2) % 3]

        def go(w, _):
            u = w // 2

            @pl.when((least(color, a, u) + 3 * (w % 2) <= 3) & (u != b))
            def _():
                for copy in second(color, u, w % 2):
                    copy.wait_send()
            return 0

        lax.fori_loop(0, 8, go, 0)
        for half in range(2):
            v = least(color, a, b) + 3 * half

            @pl.when((v <= 3) & (v != c))
            def _():
                for copy in third(color, half, v):
                    copy.wait_send()


def merge_parts(values, side):
    vmem = pl.BlockSpec(memory_space=pltpu.VMEM)
    dma = pltpu.SemaphoreType.DMA

    def both(*lead):
        return [pltpu.VMEM((*lead, 2, 128, 128), jnp.int16), pltpu.VMEM((*lead, 2, 8, 128), jnp.float32)]

    return pl.pallas_call(
        merge_kernel,
        out_shape=jax.ShapeDtypeStruct((4, 64, 128), jnp.bfloat16),
        in_specs=[vmem, vmem],
        out_specs=vmem,
        scratch_shapes=[
            *both(3, 3, 8), *both(3, 8), *both(3, 3, 2), *both(3, 2), *both(3),
            pltpu.VMEM((2, 4, 32, 128), jnp.float32), pltpu.VMEM((4, 32, 128), jnp.float32), pltpu.VMEM((4, 64, 128), jnp.float32),
            dma((3, 3, 8, 2)), dma((3, 3, 8, 2)), dma((3, 3, 2, 2)), dma((3, 3, 2, 2)), dma((3, 3, 2)), dma((3, 2)), dma((2,)),
        ],
        compiler_params=pltpu.CompilerParams(collective_id=1, has_side_effects=True, vmem_limit_bytes=48 * 2**20),
        name="merge_parts",
    )(values, side)


def local(queries, suffix_k, suffix_v, pool_k, pool_v, list_holder, list_slot, list_valid):
    lists = jnp.zeros((8, 128), jnp.int32).at[0:3, 0:8].set(jnp.stack([list_holder[:, 0], list_slot, list_valid]))
    gathered, every_list = gather_queries(queries, lists)
    keys = jnp.transpose(pool_k, (0, 2, 1, 3))
    values = jnp.transpose(pool_v, (0, 2, 3, 1))
    near_k = jnp.pad(jnp.transpose(suffix_k, (1, 0, 2)), ((0, 0), (0, 8), (0, 0)))
    near_v = jnp.concatenate([jnp.transpose(suffix_v, (1, 2, 0)), jnp.ones((4, 16, 8), jnp.bfloat16)], axis=1)
    near_v = jnp.pad(near_v, ((0, 0), (0, 0), (0, 120)))
    parts, side = attend(every_list, gathered.reshape(64, 256, 128), keys, values, near_k, near_v)
    return merge_parts(parts, side)


def solution(mesh):
    in_specs = (
        P(("store", "ctx", "head"), None, None),
        P(("store", "ctx"), "head", None),
        P(("store", "ctx"), "head", None),
        P(("store", "ctx"), None, "head", None),
        P(("store", "ctx"), None, "head", None),
        P(("store", "ctx"), None),
        P(("store", "ctx")),
        P(("store", "ctx")),
    )
    out_specs = P(("store", "ctx", "head"), None, None)
    return jax.shard_map(local, mesh=mesh, in_specs=in_specs, out_specs=out_specs, check_vma=False)
```

```python
import functools
import math

import jax
import jax.numpy as jnp
from jax import lax
from jax.experimental import pallas as pl
from jax.experimental.pallas import tpu as pltpu
from jax.sharding import PartitionSpec as P

NEG = -1e30
EXP2_SCALE = math.log2(math.e) / math.sqrt(128)
NT = (((1,), (1,)), ((), ()))
NN = (((1,), (0,)), ((), ()))
MESH = pl.DeviceIdType.MESH
PARTS = ((0, 80), (80, 80), (160, 96))
JOBS = 12
TOP16 = 32767.0


def matmul(a, b, dims=NN):
    return lax.dot_general(a, b, dims, preferred_element_type=jnp.float32)


def position():
    ctx = lax.axis_index("ctx")
    return [lax.axis_index("store"), ctx // 4, ctx % 4], lax.axis_index("head")


def device(place, core):
    return (place[0], place[1] * 4 + place[2], core)


def along(place, axis, step):
    moved = list(place)
    moved[axis] = (place[axis] + step) % 4
    return moved


def greet(place, core):
    barrier = pltpu.get_barrier_semaphore()
    for axis in range(3):
        for step in (1, 2, 3):
            pl.semaphore_signal(barrier, 1, device_id=device(along(place, axis, step), core), device_id_type=MESH)
    pl.semaphore_signal(barrier, 1, device_id=device(place, 1 - core), device_id_type=MESH)
    pl.semaphore_wait(barrier, 10)


def gather_kernel(q_ref, holder_ref, slot_ref, valid_ref, pk_ref, pv_ref, all_ref, lists_ref, kp_ref, vp_ref,
                  list_ref, theirs, send, own, raw_k, raw_v, keys, values, wide_k, wide_v,
                  swap_sem, list_sem, own_sem, send_sem, recv_sem, raw_sem, out_sem):
    place, core = position()

    def raw_copies(n):
        return [pltpu.make_async_copy(pk_ref.at[n], raw_k.at[n], raw_sem.at[0, n]),
                pltpu.make_async_copy(pv_ref.at[n], raw_v.at[n], raw_sem.at[1, n])]

    def out_copies(n):
        return [pltpu.make_async_copy(keys.at[n], kp_ref.at[n], out_sem.at[0, n]),
                pltpu.make_async_copy(values.at[n], vp_ref.at[n], out_sem.at[1, n])]

    def over(first, last, function):
        def go(n, _):
            function(n)
            return 0
        lax.fori_loop(first, last, go, 0)

    def begin(n):
        for copy in raw_copies(n):
            copy.start()

    over(0, 16, begin)
    row = lax.broadcasted_iota(jnp.int32, (8, 128), 0)
    lane = lax.broadcasted_iota(jnp.int32, (8, 128), 1)
    tile = jnp.zeros((8, 128), jnp.int32)
    for e in range(8):
        for r, ref in enumerate((holder_ref, slot_ref, valid_ref)):
            tile = jnp.where((row == r) & (lane == e), ref[e], tile)
    list_ref[...] = tile
    greet(place, core)
    swap = pltpu.make_async_remote_copy(
        q_ref.at[:, pl.ds((1 - core) * 32, 32), :], theirs, swap_sem.at[0], swap_sem.at[1],
        device_id=device(place, 1 - core), device_id_type=MESH)
    swap.start()
    lists = []
    for step in (1, 2, 3):
        copy = pltpu.make_async_remote_copy(
            list_ref, lists_ref.at[place[0]], list_sem.at[0, step - 1], list_sem.at[1, step - 1],
            device_id=device(along(place, 0, step), core), device_id_type=MESH)
        copy.start()
        lists.append(copy)
    own_lists = pltpu.make_async_copy(list_ref, lists_ref.at[place[0]], own_sem.at[1])
    own_lists.start()

    def grouped(tokens):
        wide = tokens.astype(jnp.float32).reshape(4, 4, 8, 128)
        return jnp.stack([wide[:, g].reshape(32, 128) for g in range(4)]).astype(jnp.bfloat16)

    def regroup(n):
        for copy in raw_copies(n):
            copy.wait()
        wide_k[...] = raw_k[n].astype(jnp.float32)
        wide_v[...] = raw_v[n].astype(jnp.float32)
        for g in range(4):
            keys[n, g] = wide_k[pl.ds(g, 256, stride=4), :].astype(jnp.bfloat16)
            values[n, g] = jnp.transpose(wide_v[pl.ds(g, 256, stride=4), :]).astype(jnp.bfloat16)
        for copy in out_copies(n):
            copy.start()

    send[:, pl.ds(core * 32, 32), :] = grouped(q_ref[:, pl.ds(core * 32, 32), :])
    swap.wait()
    send[:, pl.ds((1 - core) * 32, 32), :] = grouped(theirs[...])
    own[...] = send[...].reshape(256, 128)
    keep = pltpu.make_async_copy(own, all_ref.at[place[0], place[1], place[2]], own_sem.at[0])
    keep.start()

    def copies(part, phase):
        order = [(part + i) % 3 for i in range(3)]
        rows = pl.ds(*PARTS[part])
        where = [slice(None) if axis in order[:phase] else place[axis] for axis in range(3)]
        block = all_ref.at[where[0], where[1], where[2], rows]
        source = own.at[rows] if phase == 0 else block
        return [
            pltpu.make_async_remote_copy(
                source, block, send_sem.at[part, phase, step - 1], recv_sem.at[part, phase, step - 1],
                device_id=device(along(place, order[phase], step), core), device_id_type=MESH)
            for step in (1, 2, 3)
        ]

    started = []
    for phase in range(3):
        for part in range(3):
            if phase:
                for copy in started[(phase - 1) * 3 + part]:
                    copy.wait_recv()
            if phase == 1 and part == 0:
                keep.wait()
            now = copies(part, phase)
            for copy in now:
                copy.start()
            started.append(now)
        over(*((0, 3), (3, 7), (7, 16))[phase], regroup)
    for part in range(3):
        for copy in started[6 + part]:
            copy.wait_recv()
    for group in started:
        for copy in group:
            copy.wait_send()
    for copy in lists:
        copy.wait()
    own_lists.wait()

    def finish(n):
        for copy in out_copies(n):
            copy.wait()

    over(0, 16, finish)


def gather_queries(queries, holder, slot, valid, pool_k, pool_v):
    hbm = pl.BlockSpec(memory_space=pl.ANY)
    vmem, smem = pl.BlockSpec(memory_space=pltpu.VMEM), pl.BlockSpec(memory_space=pltpu.SMEM)
    dma = pltpu.SemaphoreType.DMA
    return pl.pallas_call(
        gather_kernel,
        out_shape=[
            jax.ShapeDtypeStruct((4, 4, 4, 256, 128), jnp.bfloat16), jax.ShapeDtypeStruct((4, 8, 128), jnp.int32),
            jax.ShapeDtypeStruct((16, 4, 256, 128), jnp.bfloat16), jax.ShapeDtypeStruct((16, 4, 128, 256), jnp.bfloat16),
        ],
        in_specs=[vmem, smem, smem, smem, hbm, hbm],
        out_specs=[hbm] * 4,
        scratch_shapes=[
            pltpu.VMEM((8, 128), jnp.int32), pltpu.VMEM((4, 32, 128), jnp.bfloat16),
            pltpu.VMEM((4, 64, 128), jnp.bfloat16), pltpu.VMEM((256, 128), jnp.bfloat16),
            pltpu.VMEM((16, 1024, 128), jnp.bfloat16), pltpu.VMEM((16, 1024, 128), jnp.bfloat16),
            pltpu.VMEM((16, 4, 256, 128), jnp.bfloat16), pltpu.VMEM((16, 4, 128, 256), jnp.bfloat16),
            pltpu.VMEM((1024, 128), jnp.float32), pltpu.VMEM((1024, 128), jnp.float32),
            dma((2,)), dma((2, 3)), dma((2,)), dma((3, 3, 3)), dma((3, 3, 3)), dma((2, 16)), dma((2, 16)),
        ],
        compiler_params=pltpu.CompilerParams(collective_id=0, has_side_effects=True, vmem_limit_bytes=62 * 2**20),
        name="gather_queries",
    )(queries, holder, slot, valid, pool_k, pool_v)


def attend_kernel(list_ref, q_ref, pk_ref, pv_ref, near_k_ref, near_v_ref, o_ref, side_ref,
                  kj, vj, sk_ref, sv_ref, near, peak, acc, jobs, count, sem):
    @pl.when(pl.program_id(0) == 0)
    def prepare():
        store = lax.axis_index("store")
        count[0] = 0
        count[1] = 0

        def look(i, _):
            row, e = i // 8, i % 8
            slot, valid = list_ref[row, 1, e], list_ref[row, 2, e]

            @pl.when((list_ref[row, 0, e] == store) & (valid > 0))
            def _():
                long = valid > 128
                n = jnp.where(long, count[0], JOBS - 1 - count[1])
                jobs[0, n] = slot
                jobs[1, n] = valid
                count[0] = count[0] + jnp.where(long, 1, 0)
                count[1] = count[1] + jnp.where(long, 0, 1)
                pltpu.make_async_copy(pk_ref.at[slot], kj.at[n], sem.at[0, n]).start()
                pltpu.make_async_copy(pv_ref.at[slot], vj.at[n, :, 0:128], sem.at[1, n]).start()
            return 0

        lax.fori_loop(0, 32, look, 0)
        near[0] = near_k_ref[...].astype(jnp.float32)
        near[1] = near_v_ref[...].astype(jnp.float32)
        ones = jnp.where(lax.broadcasted_iota(jnp.int32, (16, 128), 1) < 8, 1.0, 0.0)
        for g in range(4):
            k, v = near[0, pl.ds(g, 8, stride=4), :], near[1, pl.ds(g, 8, stride=4), :]
            sk_ref[g] = jnp.concatenate([k, jnp.zeros((8, 128), jnp.float32)], axis=0).astype(jnp.bfloat16)
            v = jnp.transpose(jnp.concatenate([v, jnp.zeros((120, 128), jnp.float32)], axis=0))
            sv_ref[g] = jnp.concatenate([v, ones], axis=0).astype(jnp.bfloat16)

        def fix(n, _):
            slot, valid = jobs[0, n], jobs[1, n]
            pltpu.make_async_copy(pk_ref.at[slot], kj.at[n], sem.at[0, n]).wait()
            pltpu.make_async_copy(pv_ref.at[slot], vj.at[n, :, 0:128], sem.at[1, n]).wait()
            live_row = lax.broadcasted_iota(jnp.int32, (256, 128), 0) < valid
            live_lane = lax.broadcasted_iota(jnp.int32, (128, 256), 1) < valid
            for g in range(4):
                keys = kj[n, g].astype(jnp.float32)
                kj[n, g] = jnp.where(live_row, keys, keys[0:1]).astype(jnp.bfloat16)
                vj[n, g, 0:128] = jnp.where(live_lane, vj[n, g, 0:128].astype(jnp.float32), 0.0).astype(jnp.bfloat16)
                vj[n, g, 128:144] = live_lane[0:16].astype(jnp.float32).astype(jnp.bfloat16)
            return 0

        lax.fori_loop(0, count[0], fix, 0)
        lax.fori_loop(JOBS - count[1], JOBS, fix, 0)

    pair = pl.program_id(0)
    suffix_at = (lax.axis_index("store") * 16 + lax.axis_index("ctx")) * 8
    key_at = suffix_at + lax.broadcasted_iota(jnp.int32, (8, 4096), 0)
    query_at = lax.broadcasted_iota(jnp.int32, (8, 4096), 1) // 8
    live = key_at <= query_at
    for half in range(2):
        q = q_ref[:, half * 64:(half + 1) * 64, :].reshape(4096, 128)
        s = matmul(sk_ref[pair * 2 + half], q, NT)[0:8]
        s = jnp.where(live, s, NEG)
        t = jnp.max(s, axis=0, keepdims=True)
        w = jnp.where(live, jnp.exp2((s - t) * EXP2_SCALE), 0.0)
        w = jnp.concatenate([w, jnp.zeros((120, 4096), jnp.float32)], axis=0).astype(jnp.bfloat16)
        acc[half] = matmul(sv_ref[pair * 2 + half], w)
        peak[half] = t

        def unit(first, number, keys):
            stack = kj[pl.ds(first, number), pair * 2 + half, 0:keys, :].reshape(number * keys, 128)
            s = matmul(stack, q, NT)
            m = peak[half]
            tops, terms = [], []
            for i in range(number):
                part = s[i * keys:(i + 1) * keys]
                t = jnp.max(part, axis=0, keepdims=True)
                w = jnp.exp2((part - t) * EXP2_SCALE).astype(jnp.bfloat16)
                terms.append(matmul(vj[first + i, pair * 2 + half, :, 0:keys], w))
                tops.append(t)
            top = functools.reduce(jnp.maximum, tops, m)
            new = acc[half] * jnp.exp2((m - top) * EXP2_SCALE)
            for t, x in zip(tops, terms):
                new = new + x * jnp.exp2((t - top) * EXP2_SCALE)
            acc[half] = new
            peak[half] = top

        def units(first, many, number, keys):
            def go(i, _):
                unit(first + i * number, number, keys)
                return 0

            lax.fori_loop(0, many, go, 0)

        long, short = count[0], count[1]
        units(0, long // 2, 2, 256)
        units(long - long % 2, long % 2, 1, 256)
        units(JOBS - short, short // 2, 2, 128)
        units(JOBS - 1, short % 2, 1, 128)

    low = lax.broadcasted_iota(jnp.int32, (1, 128), 1) < 64

    def emit(i, _):
        lanes = pl.ds(pl.multiple_of(i * 128, 128), 128)
        a, b = acc[0, 0:136, lanes], acc[1, 0:136, lanes]
        pa, pb = peak[0, :, lanes], peak[1, :, lanes]
        for odd in range(2):
            if odd:
                whole = jnp.where(low, pltpu.roll(a, 64, 1), b)
                top = jnp.where(low, pltpu.roll(jnp.broadcast_to(pa, (8, 128)), 64, 1)[0:1], pb)
            else:
                whole = jnp.where(low, a, pltpu.roll(b, 64, 1))
                top = jnp.where(low, pa, pltpu.roll(jnp.broadcast_to(pb, (8, 128)), 64, 1)[0:1])
            values, scale = encode(whole[0:128])
            o_ref[i * 2 + odd, 0] = values
            side_ref[i * 2 + odd, pl.ds(pair * 4, 4), :] = jnp.concatenate([top, whole[128:129], scale, scale], axis=0)
        return 0

    lax.fori_loop(0, 32, emit, 0)


def encode(x):
    largest = jnp.maximum(jnp.max(jnp.abs(x), axis=0, keepdims=True), 1e-30)
    whole = jnp.round(x * (TOP16 / largest)).astype(jnp.int32).astype(jnp.int16)
    return whole, largest * (1.0 / TOP16)


def attend(lists, gathered, pool_k, pool_v, suffix_k, suffix_v):
    hbm = pl.BlockSpec(memory_space=pl.ANY)
    return pl.pallas_call(
        attend_kernel,
        grid=(2,),
        in_specs=[
            pl.BlockSpec(memory_space=pltpu.SMEM),
            pl.BlockSpec((64, 128, 128), lambda i: (0, i, 0)),
            hbm, hbm,
            pl.BlockSpec((32, 128), lambda i: (0, 0)),
            pl.BlockSpec((32, 128), lambda i: (0, 0)),
        ],
        out_specs=[pl.BlockSpec((64, 1, 128, 128), lambda i: (0, i, 0, 0)), pl.BlockSpec((64, 8, 128), lambda i: (0, 0, 0))],
        out_shape=[jax.ShapeDtypeStruct((64, 2, 128, 128), jnp.int16), jax.ShapeDtypeStruct((64, 8, 128), jnp.float32)],
        scratch_shapes=[
            pltpu.VMEM((JOBS, 4, 256, 128), jnp.bfloat16), pltpu.VMEM((JOBS, 4, 144, 256), jnp.bfloat16),
            pltpu.VMEM((4, 16, 128), jnp.bfloat16), pltpu.VMEM((4, 144, 128), jnp.bfloat16), pltpu.VMEM((2, 32, 128), jnp.float32),
            pltpu.VMEM((2, 1, 4096), jnp.float32), pltpu.VMEM((2, 144, 4096), jnp.float32),
            pltpu.SMEM((2, JOBS), jnp.int32), pltpu.SMEM((2,), jnp.int32), pltpu.SemaphoreType.DMA((2, JOBS)),
        ],
        compiler_params=pltpu.CompilerParams(vmem_limit_bytes=62 * 2**20),
        name="attend",
    )(lists, gathered, pool_k, pool_v, suffix_k, suffix_v)


def merge(parts):
    top = functools.reduce(jnp.maximum, [side[0:1] for _, side in parts])
    total, weighted = 0.0, 0.0
    for values, side in parts:
        factor = jnp.exp2((side[0:1] - top) * EXP2_SCALE)
        total = total + side[1:2] * factor
        weighted = weighted + values.astype(jnp.int32).astype(jnp.float32) * (side[2:3] * factor)
    return weighted, top, total


def merge_kernel(o_ref, side_ref, out_ref, p0, p0s, r1, r1s, p1, p1s, r2, r2s, p2, p2s, r3, r3s, rows, swapped, wide,
                 send1, recv1, send2, recv2, send3, recv3, swap_sem, own_sem):
    place, core = position()

    def least(color, a, u):
        return (color - a - u + 9) % 3

    def number(color, a, u, v):
        at = [None] * 3
        for axis, value in zip([(color + i) % 3 for i in range(3)], (a, u, v)):
            at[axis] = value
        return at[0] * 16 + at[1] * 4 + at[2]

    def two(source, source_side, target, target_side, send, recv, to):
        return [
            pltpu.make_async_remote_copy(source, target, send.at[0], recv.at[0], device_id=to, device_id_type=MESH),
            pltpu.make_async_remote_copy(source_side, target_side, send.at[1], recv.at[1], device_id=to, device_id_type=MESH),
        ]

    def first(color, step, w):
        a = (place[color] + step) % 4
        u = w // 2
        v = least(color, a, u) + 3 * (w % 2)
        chunk = jnp.minimum(number(color, a, u, v), 63)
        return v <= 3, two(
            o_ref.at[chunk], side_ref.at[chunk], r1.at[color, step - 1, w], r1s.at[color, step - 1, w],
            send1.at[color, step - 1, w], recv1.at[color, step - 1, w], device(along(place, color, step), core))

    def each(function):
        def go(w, _):
            for step in (2, 1, 3):
                for color in range(3):
                    there, copies = first(color, step, w)

                    @pl.when(there)
                    def _():
                        for copy in copies:
                            function(copy)
            return 0
        lax.fori_loop(0, 8, go, 0)

    def own(color, w):
        u = w // 2
        v = least(color, place[color], u) + 3 * (w % 2)
        chunk = jnp.minimum(number(color, place[color], u, v), 63)
        return v <= 3, [pltpu.make_async_copy(o_ref.at[chunk], p0.at[color, w], own_sem.at[color, w, 0]),
                        pltpu.make_async_copy(side_ref.at[chunk], p0s.at[color, w], own_sem.at[color, w, 1])]

    def fetch(w, _):
        for color in range(3):
            there, copies = own(color, w)

            @pl.when(there)
            def _():
                for copy in copies:
                    copy.start()
        return 0

    greet(place, core)
    each(lambda copy: copy.start())
    lax.fori_loop(0, 8, fetch, 0)

    def second(color, u, half):
        axis = (color + 1) % 3
        step = (u - place[axis] + 4) % 4
        to = list(place)
        to[axis] = u
        at = jnp.maximum(step - 1, 0)
        return two(p1.at[color, u * 2 + half], p1s.at[color, u * 2 + half], r2.at[color, at, half], r2s.at[color, at, half],
                   send2.at[color, at, half], recv2.at[color, at, half], device(to, core))

    def fold(sources, target, target_side):
        for pair in range(2):
            weighted, top, total = merge([(values[pair], side[pair * 4:pair * 4 + 4]) for values, side in sources])
            values, scale = encode(weighted)
            target[pair] = values
            target_side[pair * 4:pair * 4 + 4] = jnp.concatenate([top, total, scale, scale], axis=0)

    for color in range(3):
        a = place[color]
        second_at = place[(color + 1) % 3]

        def go(w, _):
            u = w // 2
            v = least(color, a, u) + 3 * (w % 2)

            @pl.when(v <= 3)
            def _():
                for step in (1, 2, 3):
                    for copy in first(color, step, w)[1]:
                        copy.wait_recv()
                for copy in own(color, w)[1]:
                    copy.wait()
                fold([(p0.at[color, w], p0s.at[color, w])]
                     + [(r1.at[color, k, w], r1s.at[color, k, w]) for k in range(3)],
                     p1.at[color, w], p1s.at[color, w])

                @pl.when(u != second_at)
                def _():
                    for copy in second(color, u, w % 2):
                        copy.start()
            return 0

        lax.fori_loop(0, 8, go, 0)

    def third(color, half, v):
        axis = (color + 2) % 3
        at = jnp.maximum((v - place[axis] + 4) % 4 - 1, 0)
        to = list(place)
        to[axis] = v
        return two(p2.at[color, half], p2s.at[color, half], r3.at[at], r3s.at[at],
                   send3.at[color, at], recv3.at[at], device(to, core))

    for color in range(3):
        a, b, c = place[color], place[(color + 1) % 3], place[(color + 2) % 3]
        for half in range(2):
            v = least(color, a, b) + 3 * half

            @pl.when(v <= 3)
            def _():
                for k in range(3):
                    for copy in two(p1.at[color, 0], p1s.at[color, 0], r2.at[color, k, half], r2s.at[color, k, half],
                                    send2.at[color, k, half], recv2.at[color, k, half], device(along(place, (color + 1) % 3, 1), core)):
                        copy.wait_recv()
                slot = b * 2 + half
                fold([(p1.at[color, slot], p1s.at[color, slot])]
                     + [(r2.at[color, k, half], r2s.at[color, k, half]) for k in range(3)],
                     p2.at[color, half], p2s.at[color, half])

                @pl.when(v != c)
                def _():
                    for copy in third(color, half, v):
                        copy.start()

    color = (place[0] + place[1] + place[2]) % 3
    for k in range(3):
        for copy in two(p2.at[0, 0], p2s.at[0, 0], r3.at[k], r3s.at[k], send3.at[0, k], recv3.at[k],
                        device(along(place, 0, 1), core)):
            copy.wait_recv()
    third_at = jnp.where(color == 0, place[2], jnp.where(color == 1, place[0], place[1]))
    half = third_at // 3
    mine = [(p2.at[color, half], p2s.at[color, half])] + [(r3.at[k], r3s.at[k]) for k in range(3)]
    for pair in range(2):
        weighted, top, total = merge([(values[pair], side[pair * 4:pair * 4 + 4]) for values, side in mine])
        done = jnp.transpose(weighted / total)
        for g in range(2):
            for owner in range(2):
                rows[owner, pair * 2 + g] = done[g * 64 + owner * 32:g * 64 + (owner + 1) * 32]
    swap = pltpu.make_async_remote_copy(rows.at[1 - core], swapped, swap_sem.at[0], swap_sem.at[1],
                                        device_id=device(place, 1 - core), device_id_type=MESH)
    swap.start()

    def tokens(grouped):
        split = grouped.reshape(4, 4, 8, 128)
        return jnp.stack([jnp.concatenate([split[g, t] for g in range(4)], axis=0) for t in range(4)])

    wide[:, pl.ds(pl.multiple_of(core * 32, 32), 32), :] = tokens(rows[core])
    swap.wait()
    wide[:, pl.ds(pl.multiple_of((1 - core) * 32, 32), 32), :] = tokens(swapped[...])
    out_ref[...] = wide[...].astype(jnp.bfloat16)

    each(lambda copy: copy.wait_send())
    for color in range(3):
        a, b, c = place[color], place[(color + 1) % 3], place[(color + 2) % 3]

        def go(w, _):
            u = w // 2

            @pl.when((least(color, a, u) + 3 * (w % 2) <= 3) & (u != b))
            def _():
                for copy in second(color, u, w % 2):
                    copy.wait_send()
            return 0

        lax.fori_loop(0, 8, go, 0)
        for half in range(2):
            v = least(color, a, b) + 3 * half

            @pl.when((v <= 3) & (v != c))
            def _():
                for copy in third(color, half, v):
                    copy.wait_send()


def merge_parts(values, side):
    hbm, vmem = pl.BlockSpec(memory_space=pl.ANY), pl.BlockSpec(memory_space=pltpu.VMEM)
    dma = pltpu.SemaphoreType.DMA

    def both(*lead):
        return [pltpu.VMEM((*lead, 2, 128, 128), jnp.int16), pltpu.VMEM((*lead, 8, 128), jnp.float32)]

    return pl.pallas_call(
        merge_kernel,
        out_shape=jax.ShapeDtypeStruct((4, 64, 128), jnp.bfloat16),
        in_specs=[hbm, hbm],
        out_specs=vmem,
        scratch_shapes=[
            *both(3, 8), *both(3, 3, 8), *both(3, 8), *both(3, 3, 2), *both(3, 2), *both(3),
            pltpu.VMEM((2, 4, 32, 128), jnp.float32), pltpu.VMEM((4, 32, 128), jnp.float32), pltpu.VMEM((4, 64, 128), jnp.float32),
            dma((3, 3, 8, 2)), dma((3, 3, 8, 2)), dma((3, 3, 2, 2)), dma((3, 3, 2, 2)), dma((3, 3, 2)), dma((3, 2)), dma((2,)), dma((3, 8, 2)),
        ],
        compiler_params=pltpu.CompilerParams(collective_id=1, has_side_effects=True, vmem_limit_bytes=62 * 2**20),
        name="merge_parts",
    )(values, side)


def local(queries, suffix_k, suffix_v, pool_k, pool_v, list_holder, list_slot, list_valid):
    pool_k, pool_v = pool_k.reshape(16, 1024, 128), pool_v.reshape(16, 1024, 128)
    gathered, lists, keys, values = gather_queries(queries, list_holder.reshape(8), list_slot, list_valid, pool_k, pool_v)
    near = suffix_k.reshape(32, 128), suffix_v.reshape(32, 128)
    parts, side = attend(lists, gathered.reshape(64, 256, 128), keys, values, *near)
    return merge_parts(parts, side)


def solution(mesh):
    in_specs = (
        P(("store", "ctx", "head"), None, None),
        P(("store", "ctx"), "head", None),
        P(("store", "ctx"), "head", None),
        P(("store", "ctx"), None, "head", None),
        P(("store", "ctx"), None, "head", None),
        P(("store", "ctx"), None),
        P(("store", "ctx")),
        P(("store", "ctx")),
    )
    out_specs = P(("store", "ctx", "head"), None, None)
    return jax.shard_map(local, mesh=mesh, in_specs=in_specs, out_specs=out_specs, check_vma=False)
```

```python
import functools
import math

import jax
import jax.numpy as jnp
from jax import lax
from jax.experimental import pallas as pl
from jax.experimental.pallas import tpu as pltpu
from jax.sharding import PartitionSpec as P

NEG = -1e30
EXP2_SCALE = math.log2(math.e) / math.sqrt(128)
NT = (((1,), (1,)), ((), ()))
NN = (((1,), (0,)), ((), ()))
MESH = pl.DeviceIdType.MESH
PARTS = ((0, 48, 32), (80, 32, 48), (160, 48, 48))
SPLIT = ((0, 1, 0, 80), (1, 1, 0, 80), (0, 2, 80, 48))
JOBS = 12
SIZES = (256, 192, 128)
TOP16 = 32767.0


def matmul(a, b, dims=NN):
    return lax.dot_general(a, b, dims, preferred_element_type=jnp.float32)


def position():
    ctx = lax.axis_index("ctx")
    return [lax.axis_index("store"), ctx // 4, ctx % 4], lax.axis_index("head")


def device(place, core):
    return (place[0], place[1] * 4 + place[2], core)


def along(place, axis, step):
    moved = list(place)
    moved[axis] = (place[axis] + step) % 4
    return moved


def greet(place, core):
    barrier = pltpu.get_barrier_semaphore()
    for axis in range(3):
        for step in (1, 2, 3):
            pl.semaphore_signal(barrier, 1, device_id=device(along(place, axis, step), core), device_id_type=MESH)
    pl.semaphore_signal(barrier, 1, device_id=device(place, 1 - core), device_id_type=MESH)
    pl.semaphore_wait(barrier, 10)


def gather_kernel(q_ref, holder_ref, slot_ref, valid_ref, pk_ref, pv_ref, all_ref, lists_ref, kp_ref, vp_ref,
                  list_ref, theirs, send, own, raw_k, raw_v, keys, values, wide_k, wide_v,
                  swap_sem, list_sem, own_sem, send_sem, recv_sem, raw_sem, out_sem):
    place, core = position()

    def raw_copies(n):
        return [pltpu.make_async_copy(pk_ref.at[n], raw_k.at[n], raw_sem.at[0, n]),
                pltpu.make_async_copy(pv_ref.at[n], raw_v.at[n], raw_sem.at[1, n])]

    def out_copies(n):
        return [pltpu.make_async_copy(keys.at[n], kp_ref.at[n], out_sem.at[0, n]),
                pltpu.make_async_copy(values.at[n], vp_ref.at[n], out_sem.at[1, n])]

    def over(first, last, function):
        def go(n, _):
            function(n)
            return 0
        lax.fori_loop(first, last, go, 0)

    def begin(n):
        for copy in raw_copies(n):
            copy.start()

    over(0, 16, begin)
    row = lax.broadcasted_iota(jnp.int32, (8, 128), 0)
    lane = lax.broadcasted_iota(jnp.int32, (8, 128), 1)
    tile = jnp.zeros((8, 128), jnp.int32)
    for e in range(8):
        for r, ref in enumerate((holder_ref, slot_ref, valid_ref)):
            tile = jnp.where((row == r) & (lane == e), ref[e], tile)
    list_ref[...] = tile
    greet(place, core)
    swap = pltpu.make_async_remote_copy(
        q_ref.at[:, pl.ds((1 - core) * 32, 32), :], theirs, swap_sem.at[0], swap_sem.at[1],
        device_id=device(place, 1 - core), device_id_type=MESH)
    swap.start()
    lists = []
    for step in (1, 2, 3):
        copy = pltpu.make_async_remote_copy(
            list_ref, lists_ref.at[place[0]], list_sem.at[0, step - 1], list_sem.at[1, step - 1],
            device_id=device(along(place, 0, step), core), device_id_type=MESH)
        copy.start()
        lists.append(copy)
    own_lists = pltpu.make_async_copy(list_ref, lists_ref.at[place[0]], own_sem.at[1])
    own_lists.start()

    def grouped(tokens):
        wide = tokens.astype(jnp.float32).reshape(4, 4, 8, 128)
        return jnp.stack([wide[:, g].reshape(32, 128) for g in range(4)]).astype(jnp.bfloat16)

    def regroup(n):
        for copy in raw_copies(n):
            copy.wait()
        wide_k[...] = raw_k[n].astype(jnp.float32)
        wide_v[...] = raw_v[n].astype(jnp.float32)
        for g in range(4):
            keys[n, g] = wide_k[pl.ds(g, 256, stride=4), :].astype(jnp.bfloat16)
            values[n, g] = jnp.transpose(wide_v[pl.ds(g, 256, stride=4), :]).astype(jnp.bfloat16)
        for copy in out_copies(n):
            copy.start()

    send[:, pl.ds(core * 32, 32), :] = grouped(q_ref[:, pl.ds(core * 32, 32), :])
    swap.wait()
    send[:, pl.ds((1 - core) * 32, 32), :] = grouped(theirs[...])
    own[...] = send[...].reshape(256, 128)
    keep = pltpu.make_async_copy(own, all_ref.at[place[0], place[1], place[2]], own_sem.at[0])
    keep.start()

    def links(part, phase):
        order = [(part + i) % 3 for i in range(3)]
        axis, (at, upper, lower) = order[phase], PARTS[part]
        halves = pl.ds(at, upper), pl.ds(at + upper, lower)
        plan = ((0, 1, 0), (1, 3, 0), (1, 1, 0), (0, 3, 0), (0, 1, 3), (1, 3, 1))
        copies = []
        for i, (half, step, origin) in enumerate(plan):
            source = along(place, axis, origin)
            where = [slice(None) if d in order[:phase] else source[d] for d in range(3)]
            block = all_ref.at[where[0], where[1], where[2], halves[half]]
            copies.append(pltpu.make_async_remote_copy(
                own.at[halves[half]] if phase == 0 and origin == 0 else block, block,
                send_sem.at[part, phase, i], recv_sem.at[part, phase, i],
                device_id=device(along(place, axis, step), core), device_id_type=MESH))
        return copies

    for phase in range(3):
        for part in range(3):
            if phase:
                for i in (2, 3, 4, 5):
                    links(part, phase - 1)[i].wait_recv()
            if phase == 1 and part == 0:
                keep.wait()
            for copy in links(part, phase)[:4]:
                copy.start()
        over(*((0, 1), (2, 4), (6, 10))[phase], regroup)
        for part in range(3):
            now = links(part, phase)
            for i in (0, 1):
                now[i].wait_recv()
                now[i + 4].start()
        over(*((1, 2), (4, 6), (10, 16))[phase], regroup)
    for part in range(3):
        for i in (2, 3, 4, 5):
            links(part, 2)[i].wait_recv()
    for part in range(3):
        for phase in range(3):
            for copy in links(part, phase):
                copy.wait_send()
    for copy in lists:
        copy.wait()
    own_lists.wait()

    def finish(n):
        for copy in out_copies(n):
            copy.wait()

    over(0, 16, finish)


def gather_queries(queries, holder, slot, valid, pool_k, pool_v):
    hbm = pl.BlockSpec(memory_space=pl.ANY)
    vmem, smem = pl.BlockSpec(memory_space=pltpu.VMEM), pl.BlockSpec(memory_space=pltpu.SMEM)
    dma = pltpu.SemaphoreType.DMA
    return pl.pallas_call(
        gather_kernel,
        out_shape=[
            jax.ShapeDtypeStruct((4, 4, 4, 256, 128), jnp.bfloat16), jax.ShapeDtypeStruct((4, 8, 128), jnp.int32),
            jax.ShapeDtypeStruct((16, 4, 256, 128), jnp.bfloat16), jax.ShapeDtypeStruct((16, 4, 128, 256), jnp.bfloat16),
        ],
        in_specs=[vmem, smem, smem, smem, hbm, hbm],
        out_specs=[hbm] * 4,
        scratch_shapes=[
            pltpu.VMEM((8, 128), jnp.int32), pltpu.VMEM((4, 32, 128), jnp.bfloat16),
            pltpu.VMEM((4, 64, 128), jnp.bfloat16), pltpu.VMEM((256, 128), jnp.bfloat16),
            pltpu.VMEM((16, 1024, 128), jnp.bfloat16), pltpu.VMEM((16, 1024, 128), jnp.bfloat16),
            pltpu.VMEM((16, 4, 256, 128), jnp.bfloat16), pltpu.VMEM((16, 4, 128, 256), jnp.bfloat16),
            pltpu.VMEM((1024, 128), jnp.float32), pltpu.VMEM((1024, 128), jnp.float32),
            dma((2,)), dma((2, 3)), dma((2,)), dma((3, 3, 6)), dma((3, 3, 6)), dma((2, 16)), dma((2, 16)),
        ],
        compiler_params=pltpu.CompilerParams(collective_id=0, has_side_effects=True, vmem_limit_bytes=62 * 2**20),
        name="gather_queries",
    )(queries, holder, slot, valid, pool_k, pool_v)


def attend_kernel(list_ref, q_ref, pk_ref, pv_ref, near_k_ref, near_v_ref, o_ref, side_ref,
                  kj, vj, sk_ref, sv_ref, near, peak, acc, jobs, count, sem):
    @pl.when(pl.program_id(0) == 0)
    def prepare():
        store = lax.axis_index("store")
        for i in range(len(SIZES)):
            count[i] = 0

        def look(i, _):
            row, e = i // 8, i % 8
            slot, valid = list_ref[row, 1, e], list_ref[row, 2, e]

            @pl.when((list_ref[row, 0, e] == store) & (valid > 0))
            def _():
                size = jnp.where(valid > SIZES[1], 0, jnp.where(valid > SIZES[2], 1, 2))
                n = size * JOBS + count[size]
                jobs[0, n] = slot
                jobs[1, n] = valid
                count[size] = count[size] + 1
                pltpu.make_async_copy(pk_ref.at[slot], kj.at[n], sem.at[0, n]).start()
                pltpu.make_async_copy(pv_ref.at[slot], vj.at[n, :, 0:128], sem.at[1, n]).start()
            return 0

        lax.fori_loop(0, 32, look, 0)
        near[0] = near_k_ref[...].astype(jnp.float32)
        near[1] = near_v_ref[...].astype(jnp.float32)
        ones = jnp.where(lax.broadcasted_iota(jnp.int32, (16, 128), 1) < 8, 1.0, 0.0)
        for g in range(4):
            k, v = near[0, pl.ds(g, 8, stride=4), :], near[1, pl.ds(g, 8, stride=4), :]
            sk_ref[g] = jnp.concatenate([k, jnp.zeros((8, 128), jnp.float32)], axis=0).astype(jnp.bfloat16)
            v = jnp.transpose(jnp.concatenate([v, jnp.zeros((120, 128), jnp.float32)], axis=0))
            sv_ref[g] = jnp.concatenate([v, ones], axis=0).astype(jnp.bfloat16)

        def fix(n, _):
            slot, valid = jobs[0, n], jobs[1, n]
            pltpu.make_async_copy(pk_ref.at[slot], kj.at[n], sem.at[0, n]).wait()
            pltpu.make_async_copy(pv_ref.at[slot], vj.at[n, :, 0:128], sem.at[1, n]).wait()
            live_row = lax.broadcasted_iota(jnp.int32, (256, 128), 0) < valid
            live_lane = lax.broadcasted_iota(jnp.int32, (128, 256), 1) < valid
            for g in range(4):
                keys = kj[n, g].astype(jnp.float32)
                kj[n, g] = jnp.where(live_row, keys, keys[0:1]).astype(jnp.bfloat16)
                vj[n, g, 0:128] = jnp.where(live_lane, vj[n, g, 0:128].astype(jnp.float32), 0.0).astype(jnp.bfloat16)
                vj[n, g, 128:144] = live_lane[0:16].astype(jnp.float32).astype(jnp.bfloat16)
            return 0

        for i in range(len(SIZES)):
            lax.fori_loop(i * JOBS, i * JOBS + count[i], fix, 0)

    pair = pl.program_id(0)
    suffix_at = (lax.axis_index("store") * 16 + lax.axis_index("ctx")) * 8
    key_at = suffix_at + lax.broadcasted_iota(jnp.int32, (8, 4096), 0)
    query_at = lax.broadcasted_iota(jnp.int32, (8, 4096), 1) // 8
    live = key_at <= query_at
    for half in range(2):
        q = q_ref[:, half * 64:(half + 1) * 64, :].reshape(4096, 128)
        s = matmul(sk_ref[pair * 2 + half], q, NT)[0:8]
        s = jnp.where(live, s, NEG)
        t = jnp.max(s, axis=0, keepdims=True)
        w = jnp.where(live, jnp.exp2((s - t) * EXP2_SCALE), 0.0)
        w = jnp.concatenate([w, jnp.zeros((120, 4096), jnp.float32)], axis=0).astype(jnp.bfloat16)
        acc[half] = matmul(sv_ref[pair * 2 + half], w)
        peak[half] = t

        def unit(first, number, keys):
            stack = kj[pl.ds(first, number), pair * 2 + half, 0:keys, :].reshape(number * keys, 128)
            s = matmul(stack, q, NT)
            m = peak[half]
            tops, terms = [], []
            for i in range(number):
                part = s[i * keys:(i + 1) * keys]
                t = jnp.max(part, axis=0, keepdims=True)
                w = jnp.exp2((part - t) * EXP2_SCALE).astype(jnp.bfloat16)
                terms.append(matmul(vj[first + i, pair * 2 + half, :, 0:keys], w))
                tops.append(t)
            top = functools.reduce(jnp.maximum, tops, m)
            new = acc[half] * jnp.exp2((m - top) * EXP2_SCALE)
            for t, x in zip(tops, terms):
                new = new + x * jnp.exp2((t - top) * EXP2_SCALE)
            acc[half] = new
            peak[half] = top

        def units(first, many, number, keys):
            def go(i, _):
                unit(first + i * number, number, keys)
                return 0

            lax.fori_loop(0, many, go, 0)

        for i, keys in enumerate(SIZES):
            many = count[i]
            units(i * JOBS, many // 2, 2, keys)
            units(i * JOBS + many - many % 2, many % 2, 1, keys)

    low = lax.broadcasted_iota(jnp.int32, (1, 128), 1) < 64

    def emit(i, _):
        lanes = pl.ds(pl.multiple_of(i * 128, 128), 128)
        a, b = acc[0, 0:136, lanes], acc[1, 0:136, lanes]
        pa, pb = peak[0, :, lanes], peak[1, :, lanes]
        for odd in range(2):
            if odd:
                whole = jnp.where(low, pltpu.roll(a, 64, 1), b)
                top = jnp.where(low, pltpu.roll(jnp.broadcast_to(pa, (8, 128)), 64, 1)[0:1], pb)
            else:
                whole = jnp.where(low, a, pltpu.roll(b, 64, 1))
                top = jnp.where(low, pa, pltpu.roll(jnp.broadcast_to(pb, (8, 128)), 64, 1)[0:1])
            values, scale = encode(whole[0:128])
            o_ref[i * 2 + odd, 0] = values
            side_ref[i * 2 + odd, pl.ds(pair * 4, 4), :] = jnp.concatenate([top, whole[128:129], scale, scale], axis=0)
        return 0

    lax.fori_loop(0, 32, emit, 0, unroll=8)


def encode(x):
    largest = jnp.maximum(jnp.max(jnp.abs(x), axis=0, keepdims=True), 1e-30)
    whole = jnp.round(x * (TOP16 / largest)).astype(jnp.int32).astype(jnp.int16)
    return whole, largest * (1.0 / TOP16)


def attend(lists, gathered, pool_k, pool_v, suffix_k, suffix_v):
    hbm = pl.BlockSpec(memory_space=pl.ANY)
    return pl.pallas_call(
        attend_kernel,
        grid=(2,),
        in_specs=[
            pl.BlockSpec(memory_space=pltpu.SMEM),
            pl.BlockSpec((64, 128, 128), lambda i: (0, i, 0)),
            hbm, hbm,
            pl.BlockSpec((32, 128), lambda i: (0, 0)),
            pl.BlockSpec((32, 128), lambda i: (0, 0)),
        ],
        out_specs=[pl.BlockSpec((64, 1, 128, 128), lambda i: (0, i, 0, 0)), pl.BlockSpec((64, 8, 128), lambda i: (0, 0, 0))],
        out_shape=[jax.ShapeDtypeStruct((64, 2, 128, 128), jnp.int16), jax.ShapeDtypeStruct((64, 8, 128), jnp.float32)],
        scratch_shapes=[
            pltpu.VMEM((3 * JOBS, 4, 256, 128), jnp.bfloat16), pltpu.VMEM((3 * JOBS, 4, 144, 256), jnp.bfloat16),
            pltpu.VMEM((4, 16, 128), jnp.bfloat16), pltpu.VMEM((4, 144, 128), jnp.bfloat16), pltpu.VMEM((2, 32, 128), jnp.float32),
            pltpu.VMEM((2, 1, 4096), jnp.float32), pltpu.VMEM((2, 144, 4096), jnp.float32),
            pltpu.SMEM((2, 3 * JOBS), jnp.int32), pltpu.SMEM((3,), jnp.int32), pltpu.SemaphoreType.DMA((2, 3 * JOBS)),
        ],
        compiler_params=pltpu.CompilerParams(vmem_limit_bytes=62 * 2**20),
        name="attend",
    )(lists, gathered, pool_k, pool_v, suffix_k, suffix_v)


def merge(parts):
    top = functools.reduce(jnp.maximum, [side[0:1] for _, side in parts])
    total, weighted = 0.0, 0.0
    for values, side in parts:
        factor = jnp.exp2((side[0:1] - top) * EXP2_SCALE)
        total = total + side[1:2] * factor
        weighted = weighted + values.astype(jnp.int32).astype(jnp.float32) * (side[2:3] * factor)
    return weighted, top, total


def merge_kernel(o_ref, side_ref, out_ref, *scratch):
    buffers = [scratch[i * 12:(i + 1) * 12] for i in range(3)]
    rows, swapped, wide, send_sem, recv_sem, own_sem, swap_sem = scratch[36:]
    place, core = position()

    def cut(part, at):
        pair, pairs, row, many = SPLIT[part]
        where = [slice(None)] * 3
        where[part] = at
        return (o_ref.at[where[0], where[1], where[2], pl.ds(pair, pairs), pl.ds(row, many)],
                side_ref.at[where[0], where[1], where[2]])

    def line(part, ref, at, other=slice(None)):
        return ref.at[other, at] if part == 1 else ref.at[at, other]

    def copies(part, stage, step):
        p0, p0s, r1, r1s, m1, m1s, r2, r2s, m2, m2s, r3, r3s = buffers[part]
        axis = (part + stage) % 3
        to = along(place, axis, step)
        if stage == 0:
            sources, targets = cut(part, to[axis]), (r1, r1s)
        elif stage == 1:
            sources, targets = (line(part, m1, to[axis]), line(part, m1s, to[axis])), (r2, r2s)
        else:
            sources, targets = (m2.at[to[axis]], m2s.at[to[axis]]), (r3, r3s)
        return [
            pltpu.make_async_remote_copy(
                source, target.at[step - 1], send_sem.at[part, stage, step - 1, i], recv_sem.at[part, stage, step - 1, i],
                device_id=device(to, core), device_id_type=MESH)
            for i, (source, target) in enumerate(zip(sources, targets))
        ]

    def start(part, stage):
        for step in (2, 1, 3):
            for copy in copies(part, stage, step):
                copy.start()

    def arrive(part, stage):
        for step in (1, 2, 3):
            for copy in copies(part, stage, step):
                copy.wait_recv()

    def combine(part, sources):
        pair, pairs = SPLIT[part][:2]
        return [merge([(values[i], side[(pair + i) * 4:(pair + i) * 4 + 4]) for values, side in sources]) for i in range(pairs)]

    def fold(part, sources, target, target_side):
        pair = SPLIT[part][0]
        sides = [jnp.zeros((4, 128), jnp.float32)] * 2
        for i, (weighted, top, total) in enumerate(combine(part, sources)):
            values, scale = encode(weighted)
            target[i] = values
            sides[pair + i] = jnp.concatenate([top, total, scale, scale], axis=0)
        target_side[...] = jnp.concatenate(sides, axis=0)

    keep = [[pltpu.make_async_copy(source, target, own_sem.at[part, i])
             for i, (source, target) in enumerate(zip(cut(part, place[part]), buffers[part][:2]))] for part in range(3)]
    for pair in keep:
        for copy in pair:
            copy.start()
    greet(place, core)
    for part in range(3):
        start(part, 0)
    for part in range(3):
        p0, p0s, r1, r1s, m1, m1s = buffers[part][:6]
        for copy in keep[part]:
            copy.wait()
        arrive(part, 0)

        def first(n, _):
            i, j = n // 4, n % 4
            fold(part, [(p0.at[i, j], p0s.at[i, j])] + [(r1.at[k, i, j], r1s.at[k, i, j]) for k in range(3)],
                 m1.at[i, j], m1s.at[i, j])
            return 0

        lax.fori_loop(0, 16, first, 0)
        start(part, 1)
    for part in range(3):
        m1, m1s, r2, r2s, m2, m2s = buffers[part][4:10]
        at = place[(part + 1) % 3]
        arrive(part, 1)

        def second(c, _):
            fold(part, [(line(part, m1, at, c), line(part, m1s, at, c))] + [(r2.at[k, c], r2s.at[k, c]) for k in range(3)],
                 m2.at[c], m2s.at[c])
            return 0

        lax.fori_loop(0, 4, second, 0)
        start(part, 2)
    pieces = [[], []]
    for part in range(3):
        m2, m2s, r3, r3s = buffers[part][8:]
        at = place[(part + 2) % 3]
        arrive(part, 2)
        sources = [(m2.at[at], m2s.at[at])] + [(r3.at[k], r3s.at[k]) for k in range(3)]
        for i, (weighted, _, total) in enumerate(combine(part, sources)):
            pieces[SPLIT[part][0] + i].append(weighted / total)
    for pair in range(2):
        done = jnp.transpose(jnp.concatenate(pieces[pair], axis=0))
        for g in range(2):
            for owner in range(2):
                rows[owner, pair * 2 + g] = done[g * 64 + owner * 32:g * 64 + (owner + 1) * 32]
    swap = pltpu.make_async_remote_copy(rows.at[1 - core], swapped, swap_sem.at[0], swap_sem.at[1],
                                        device_id=device(place, 1 - core), device_id_type=MESH)
    swap.start()

    def tokens(grouped):
        split = grouped.reshape(4, 4, 8, 128)
        return jnp.stack([jnp.concatenate([split[g, t] for g in range(4)], axis=0) for t in range(4)])

    wide[:, pl.ds(pl.multiple_of(core * 32, 32), 32), :] = tokens(rows[core])
    swap.wait()
    wide[:, pl.ds(pl.multiple_of((1 - core) * 32, 32), 32), :] = tokens(swapped[...])
    out_ref[...] = wide[...].astype(jnp.bfloat16)

    for part in range(3):
        for stage in range(3):
            for step in (1, 2, 3):
                for copy in copies(part, stage, step):
                    copy.wait_send()


def merge_parts(values, side):
    hbm, vmem = pl.BlockSpec(memory_space=pl.ANY), pl.BlockSpec(memory_space=pltpu.VMEM)
    dma = pltpu.SemaphoreType.DMA
    buffers = []
    for _, pairs, _, many in SPLIT:
        for lead in ((4, 4), (3, 4, 4), (4, 4), (3, 4), (4,), (3,)):
            buffers += [pltpu.VMEM((*lead, pairs, many, 128), jnp.int16), pltpu.VMEM((*lead, 8, 128), jnp.float32)]
    return pl.pallas_call(
        merge_kernel,
        out_shape=jax.ShapeDtypeStruct((4, 64, 128), jnp.bfloat16),
        in_specs=[hbm, hbm],
        out_specs=vmem,
        scratch_shapes=[
            *buffers,
            pltpu.VMEM((2, 4, 32, 128), jnp.float32), pltpu.VMEM((4, 32, 128), jnp.float32), pltpu.VMEM((4, 64, 128), jnp.float32),
            dma((3, 3, 3, 2)), dma((3, 3, 3, 2)), dma((3, 2)), dma((2,)),
        ],
        compiler_params=pltpu.CompilerParams(collective_id=1, has_side_effects=True, vmem_limit_bytes=62 * 2**20),
        name="merge_parts",
    )(values.reshape(4, 4, 4, 2, 128, 128), side.reshape(4, 4, 4, 8, 128))


def local(queries, suffix_k, suffix_v, pool_k, pool_v, list_holder, list_slot, list_valid):
    pool_k, pool_v = pool_k.reshape(16, 1024, 128), pool_v.reshape(16, 1024, 128)
    gathered, lists, keys, values = gather_queries(queries, list_holder.reshape(8), list_slot, list_valid, pool_k, pool_v)
    near = suffix_k.reshape(32, 128), suffix_v.reshape(32, 128)
    parts, side = attend(lists, gathered.reshape(64, 256, 128), keys, values, *near)
    return merge_parts(parts, side)


def solution(mesh):
    in_specs = (
        P(("store", "ctx", "head"), None, None),
        P(("store", "ctx"), "head", None),
        P(("store", "ctx"), "head", None),
        P(("store", "ctx"), None, "head", None),
        P(("store", "ctx"), None, "head", None),
        P(("store", "ctx"), None),
        P(("store", "ctx")),
        P(("store", "ctx")),
    )
    out_specs = P(("store", "ctx", "head"), None, None)
    return jax.shard_map(local, mesh=mesh, in_specs=in_specs, out_specs=out_specs, check_vma=False)
```

```python
import functools
import math

import jax
import jax.numpy as jnp
from jax import lax
from jax.experimental import pallas as pl
from jax.experimental.pallas import tpu as pltpu
from jax.sharding import PartitionSpec as P

NEG = -1e30
EXP2_SCALE = math.log2(math.e) / math.sqrt(128)
NT = (((1,), (1,)), ((), ()))
NN = (((1,), (0,)), ((), ()))
MESH = pl.DeviceIdType.MESH
PARTS = ((0, 48, 48), (96, 32, 32), (160, 48, 48))
SPLIT = ((0, 1, 0, 80), (1, 1, 0, 80), (0, 2, 80, 48))
ORDERS = ((0, 1, 2), (1, 2, 0), (0, 2, 1))
JOBS = 14
COSTS = (115, 90, 72)
SIZES = (256, 192, 128)
TOP16 = 32767.0


def matmul(a, b, dims=NN):
    return lax.dot_general(a, b, dims, preferred_element_type=jnp.float32)


def position():
    ctx = lax.axis_index("ctx")
    return [lax.axis_index("store"), ctx // 4, ctx % 4], lax.axis_index("head")


def device(place, core):
    return (place[0], place[1] * 4 + place[2], core)


def along(place, axis, step):
    moved = list(place)
    moved[axis] = (place[axis] + step) % 4
    return moved


def greet(place, core):
    barrier = pltpu.get_barrier_semaphore()
    for axis in range(3):
        for step in (1, 2, 3):
            pl.semaphore_signal(barrier, 1, device_id=device(along(place, axis, step), core), device_id_type=MESH)
    pl.semaphore_signal(barrier, 1, device_id=device(place, 1 - core), device_id_type=MESH)
    pl.semaphore_wait(barrier, 10)


def size_class(valid):
    return jnp.where(valid > SIZES[1], 0, jnp.where(valid > SIZES[2], 1, 2))


def pick(options, index):
    value = options[0]
    for i in range(1, len(options)):
        value = jnp.where(index == i, options[i], value)
    return value


def whole(reduce, x):
    return reduce(reduce(x, axis=1, keepdims=True), axis=0, keepdims=True)


def plan_moves(holder, valid, number):
    live = (valid > 0) & (number >= 0)
    size = size_class(valid)
    cost = jnp.where(live, pick([jnp.full_like(valid, c) for c in COSTS], size), 0)
    loads = [whole(jnp.sum, jnp.where(holder == s, cost, 0)) for s in range(4)]
    none = jnp.full((1, 1), -1, jnp.int32)
    moves = [[none, none] for _ in range(4)]
    for _ in range(5):
        most = functools.reduce(jnp.maximum, loads)
        giver = jnp.where(loads[0] == most, 0, jnp.where(loads[1] == most, 1, jnp.where(loads[2] == most, 2, 3)))
        ways = []
        for way, step in enumerate((1, 3)):
            free = pick([moves[s][way] for s in range(4)], giver) < 0
            ways.append(jnp.where(free, pick(loads[step:] + loads[:step], giver), 1 << 20))
        way = jnp.where(ways[0] <= ways[1], 0, 1)
        least = jnp.minimum(ways[0], ways[1])
        gone = [pick([moves[s][w] for s in range(4)], giver) for w in range(2)]
        at = live & (holder == giver) & (number != gone[0]) & (number != gone[1])
        found = [whole(jnp.max, jnp.where(at & (size == k), number, -1)) for k in range(3)]
        entry, saved = none, jnp.zeros((1, 1), jnp.int32)
        for k in (2, 1, 0):
            helps = (found[k] >= 0) & (least + COSTS[k] < most)
            entry, saved = jnp.where(helps, found[k], entry), jnp.where(helps, COSTS[k], saved)
        for s in range(4):
            takes = ((giver == (s + 3) % 4) & (way == 0)) | ((giver == (s + 1) % 4) & (way == 1))
            loads[s] = loads[s] - jnp.where(giver == s, saved, 0) + jnp.where(takes, saved, 0)
            for w in range(2):
                moves[s][w] = jnp.where((giver == s) & (way == w) & (entry >= 0), entry, moves[s][w])
    return moves


def gather_kernel(q_ref, holder_ref, slot_ref, valid_ref, pk_ref, pv_ref, all_ref, lists_ref, kp_ref, vp_ref, plan_ref,
                  list_ref, table, plan_tile, out_k, out_v, in_k, in_v, theirs, send, own, raw_k, raw_v, keys, values, wide_k, wide_v,
                  swap_sem, list_sem, own_sem, send_sem, recv_sem, raw_sem, out_sem, plan_sem, move_send, move_recv):
    place, core = position()

    def raw_copies(n):
        return [pltpu.make_async_copy(pk_ref.at[n], raw_k.at[n], raw_sem.at[0, n]),
                pltpu.make_async_copy(pv_ref.at[n], raw_v.at[n], raw_sem.at[1, n])]

    def out_copies(n):
        return [pltpu.make_async_copy(keys.at[n], kp_ref.at[n], out_sem.at[0, n]),
                pltpu.make_async_copy(values.at[n], vp_ref.at[n], out_sem.at[1, n])]

    def over(first, last, function):
        def go(n, _):
            function(n)
            return 0
        lax.fori_loop(first, last, go, 0)

    def begin(n):
        for copy in raw_copies(n):
            copy.start()

    over(0, 16, begin)
    row = lax.broadcasted_iota(jnp.int32, (8, 128), 0)
    lane = lax.broadcasted_iota(jnp.int32, (8, 128), 1)
    tile = jnp.zeros((8, 128), jnp.int32)
    for e in range(8):
        for r, ref in enumerate((holder_ref, slot_ref, valid_ref)):
            tile = jnp.where((row == r) & (lane == e), ref[e], tile)
    list_ref[...] = tile
    greet(place, core)
    swap = pltpu.make_async_remote_copy(
        q_ref.at[:, pl.ds((1 - core) * 32, 32), :], theirs, swap_sem.at[0], swap_sem.at[1],
        device_id=device(place, 1 - core), device_id_type=MESH)
    swap.start()
    lists = []
    for step in (1, 2, 3):
        copy = pltpu.make_async_remote_copy(
            list_ref, table.at[place[0]], list_sem.at[0, step - 1], list_sem.at[1, step - 1],
            device_id=device(along(place, 0, step), core), device_id_type=MESH)
        copy.start()
        lists.append(copy)
    own_lists = pltpu.make_async_copy(list_ref, table.at[place[0]], own_sem.at[1])
    own_lists.start()

    def grouped(tokens):
        wide = tokens.astype(jnp.float32).reshape(4, 4, 8, 128)
        return jnp.stack([wide[:, g].reshape(32, 128) for g in range(4)]).astype(jnp.bfloat16)

    def regroup(n, of_k=raw_k, of_v=raw_v, first=0):
        wide_k[...] = of_k[n - first].astype(jnp.float32)
        wide_v[...] = of_v[n - first].astype(jnp.float32)
        for g in range(4):
            keys[n, g] = wide_k[pl.ds(g, 256, stride=4), :].astype(jnp.bfloat16)
            values[n, g] = jnp.transpose(wide_v[pl.ds(g, 256, stride=4), :]).astype(jnp.bfloat16)
        for copy in out_copies(n):
            copy.start()

    send[:, pl.ds(core * 32, 32), :] = grouped(q_ref[:, pl.ds(core * 32, 32), :])
    swap.wait()
    send[:, pl.ds((1 - core) * 32, 32), :] = grouped(theirs[...])
    own[...] = send[...].reshape(256, 128)
    keep = pltpu.make_async_copy(own, all_ref.at[place[0], place[1], place[2]], own_sem.at[0])
    keep.start()

    def links(part, phase, which):
        order = ORDERS[part]
        axis, (at, upper, lower) = order[phase], PARTS[part]
        halves = pl.ds(at, upper), pl.ds(at + upper, lower)
        plan = ((0, 1, 0), (1, 3, 0), (1, 1, 0), (0, 3, 0), (0, 1, 3), (1, 3, 1))
        copies = []
        for i in which:
            half, step, origin = plan[i]
            source = along(place, axis, origin)
            where = [slice(None) if d in order[:phase] else source[d] for d in range(3)]
            block = all_ref.at[where[0], where[1], where[2], halves[half]]
            copies.append(pltpu.make_async_remote_copy(
                own.at[halves[half]] if phase == 0 and origin == 0 else block, block,
                send_sem.at[part, phase, i], recv_sem.at[part, phase, i],
                device_id=device(along(place, axis, step), core), device_id_type=MESH))
        return copies

    def move(way):
        to = device(along(place, 0, (1, 3)[way]), core)
        return [
            pltpu.make_async_remote_copy(source.at[way], target.at[way], move_send.at[way, i], move_recv.at[way, i],
                                         device_id=to, device_id_type=MESH)
            for i, (source, target) in enumerate(((out_k, in_k), (out_v, in_v)))
        ]

    def ready(n):
        for copy in raw_copies(n):
            copy.wait()

    def balance():
        for copy in lists:
            copy.wait()
        own_lists.wait()
        pltpu.make_async_copy(table, lists_ref, plan_sem.at[0]).start()
        over(0, 16, ready)
        holder, slots, valid = (table[:, i, :] for i in range(3))
        lanes = lax.broadcasted_iota(jnp.int32, (4, 128), 1)
        number = jnp.where(lanes < 8, lax.broadcasted_iota(jnp.int32, (4, 128), 0) * 8 + lanes, -1)
        moves = plan_moves(holder, valid, number)
        given = [pick([moves[s][way] for s in range(4)], place[0]) for way in range(2)]
        taken = [pick([moves[s][way] for s in range(4)], (place[0] + (3, 1)[way]) % 4) for way in range(2)]
        for way in range(2):
            slot = jnp.max(jnp.where((number == given[way]) & (number >= 0), slots, 0))
            out_k[way] = raw_k[slot]
            out_v[way] = raw_v[slot]
            for copy in move(way):
                copy.start()
        first_row = row == 0
        told = jnp.zeros((8, 128), jnp.int32)
        for i, value in enumerate(given + taken):
            told = jnp.where(first_row & (lane == i), value, told)
        plan_tile[...] = told
        pltpu.make_async_copy(plan_tile, plan_ref, plan_sem.at[1]).start()

    for phase in range(3):
        for part in range(3):
            if phase:
                for i in (2, 3, 4, 5):
                    links(part, phase - 1, (i,))[0].wait_recv()
            if phase == 1 and part == 0:
                keep.wait()
            for copy in links(part, phase, range(4)):
                copy.start()
        over(*((0, 0), (2, 4), (6, 10))[phase], regroup)
        for part in range(3):
            for i in (0, 1):
                links(part, phase, (i,))[0].wait_recv()
                links(part, phase, (i + 4,))[0].start()
        if phase == 0:
            balance()
        over(*((0, 2), (4, 6), (10, 16))[phase], regroup)
    for way in range(2):
        for copy in move(way):
            copy.wait()
    over(16, 18, functools.partial(regroup, of_k=in_k, of_v=in_v, first=16))
    for part in range(3):
        for i in (2, 3, 4, 5):
            links(part, 2, (i,))[0].wait_recv()
    for part in range(3):
        for phase in range(3):
            for copy in links(part, phase, range(6)):
                copy.wait_send()
    pltpu.make_async_copy(plan_tile, plan_ref, plan_sem.at[1]).wait()
    pltpu.make_async_copy(table, lists_ref, plan_sem.at[0]).wait()

    def finish(n):
        for copy in out_copies(n):
            copy.wait()

    over(0, 18, finish)


def gather_queries(queries, holder, slot, valid, pool_k, pool_v):
    hbm = pl.BlockSpec(memory_space=pl.ANY)
    vmem, smem = pl.BlockSpec(memory_space=pltpu.VMEM), pl.BlockSpec(memory_space=pltpu.SMEM)
    dma = pltpu.SemaphoreType.DMA
    return pl.pallas_call(
        gather_kernel,
        out_shape=[
            jax.ShapeDtypeStruct((4, 4, 4, 256, 128), jnp.bfloat16), jax.ShapeDtypeStruct((4, 8, 128), jnp.int32),
            jax.ShapeDtypeStruct((18, 4, 256, 128), jnp.bfloat16), jax.ShapeDtypeStruct((18, 4, 128, 256), jnp.bfloat16),
            jax.ShapeDtypeStruct((8, 128), jnp.int32),
        ],
        in_specs=[vmem, smem, smem, smem, hbm, hbm],
        out_specs=[hbm] * 5,
        scratch_shapes=[
            pltpu.VMEM((8, 128), jnp.int32), pltpu.VMEM((4, 8, 128), jnp.int32), pltpu.VMEM((8, 128), jnp.int32),
            *[pltpu.VMEM((2, 1024, 128), jnp.bfloat16)] * 4, pltpu.VMEM((4, 32, 128), jnp.bfloat16),
            pltpu.VMEM((4, 64, 128), jnp.bfloat16), pltpu.VMEM((256, 128), jnp.bfloat16),
            pltpu.VMEM((16, 1024, 128), jnp.bfloat16), pltpu.VMEM((16, 1024, 128), jnp.bfloat16),
            pltpu.VMEM((18, 4, 256, 128), jnp.bfloat16), pltpu.VMEM((18, 4, 128, 256), jnp.bfloat16),
            pltpu.VMEM((1024, 128), jnp.float32), pltpu.VMEM((1024, 128), jnp.float32),
            dma((2,)), dma((2, 3)), dma((2,)), dma((3, 3, 6)), dma((3, 3, 6)), dma((2, 16)), dma((2, 18)), dma((2,)), dma((2, 2)), dma((2, 2)),
        ],
        compiler_params=pltpu.CompilerParams(collective_id=0, has_side_effects=True, vmem_limit_bytes=62 * 2**20),
        name="gather_queries",
    )(queries, holder, slot, valid, pool_k, pool_v)


def attend_kernel(list_ref, plan_ref, q_ref, pk_ref, pv_ref, near_k_ref, near_v_ref, o_ref, side_ref,
                  kj, vj, sk_ref, sv_ref, near, peak, acc, jobs, count, sem):
    def starts(size):
        return (0, JOBS, JOBS - count[2])[size]

    @pl.when(pl.program_id(0) == 0)
    def prepare():
        store = lax.axis_index("store")
        for i in range(len(SIZES)):
            count[i] = 0

        def add(slot, valid):
            size = size_class(valid)
            n = jnp.where(size == 0, count[0], jnp.where(size == 1, JOBS + count[1], JOBS - 1 - count[2]))
            jobs[0, n] = slot
            jobs[1, n] = valid
            count[size] = count[size] + 1
            pltpu.make_async_copy(pk_ref.at[slot], kj.at[n], sem.at[0, n]).start()
            pltpu.make_async_copy(pv_ref.at[slot], vj.at[n, :, 0:128], sem.at[1, n]).start()

        def look(i, _):
            r, e = i // 8, i % 8
            kept = (i != plan_ref[0, 0]) & (i != plan_ref[0, 1])

            @pl.when((list_ref[r, 0, e] == store) & (list_ref[r, 2, e] > 0) & kept)
            def _():
                add(list_ref[r, 1, e], list_ref[r, 2, e])
            return 0

        for way in range(2):
            entry = plan_ref[0, 2 + way]

            @pl.when(entry >= 0)
            def _():
                add(16 + way, list_ref[entry // 8, 2, entry % 8])

        lax.fori_loop(0, 32, look, 0)
        near[0] = near_k_ref[...].astype(jnp.float32)
        near[1] = near_v_ref[...].astype(jnp.float32)
        ones = jnp.where(lax.broadcasted_iota(jnp.int32, (16, 128), 1) < 8, 1.0, 0.0)
        for g in range(4):
            k, v = near[0, pl.ds(g, 8, stride=4), :], near[1, pl.ds(g, 8, stride=4), :]
            sk_ref[g] = jnp.concatenate([k, jnp.zeros((8, 128), jnp.float32)], axis=0).astype(jnp.bfloat16)
            v = jnp.transpose(jnp.concatenate([v, jnp.zeros((120, 128), jnp.float32)], axis=0))
            sv_ref[g] = jnp.concatenate([v, ones], axis=0).astype(jnp.bfloat16)

        def fix(n, _):
            slot, valid = jobs[0, n], jobs[1, n]
            pltpu.make_async_copy(pk_ref.at[slot], kj.at[n], sem.at[0, n]).wait()
            pltpu.make_async_copy(pv_ref.at[slot], vj.at[n, :, 0:128], sem.at[1, n]).wait()
            live_row = lax.broadcasted_iota(jnp.int32, (256, 128), 0) < valid
            live_lane = lax.broadcasted_iota(jnp.int32, (128, 256), 1) < valid
            for g in range(4):
                keys = kj[n, g].astype(jnp.float32)
                kj[n, g] = jnp.where(live_row, keys, keys[0:1]).astype(jnp.bfloat16)
                vj[n, g, 0:128] = jnp.where(live_lane, vj[n, g, 0:128].astype(jnp.float32), 0.0).astype(jnp.bfloat16)
                vj[n, g, 128:144] = live_lane[0:16].astype(jnp.float32).astype(jnp.bfloat16)
            return 0

        for i in range(3):
            lax.fori_loop(starts(i), starts(i) + count[i], fix, 0)

    pair = pl.program_id(0)
    suffix_at = (lax.axis_index("store") * 16 + lax.axis_index("ctx")) * 8
    key_at = suffix_at + lax.broadcasted_iota(jnp.int32, (8, 4096), 0)
    query_at = lax.broadcasted_iota(jnp.int32, (8, 4096), 1) // 8
    live = key_at <= query_at
    for half in range(2):
        q = q_ref[:, half * 64:(half + 1) * 64, :].reshape(4096, 128)
        s = matmul(sk_ref[pair * 2 + half], q, NT)[0:8]
        s = jnp.where(live, s, NEG)
        t = jnp.max(s, axis=0, keepdims=True)
        w = jnp.where(live, jnp.exp2((s - t) * EXP2_SCALE), 0.0)
        w = jnp.concatenate([w, jnp.zeros((120, 4096), jnp.float32)], axis=0).astype(jnp.bfloat16)
        acc[half] = matmul(sv_ref[pair * 2 + half], w)
        peak[half] = t

        def unit(first, number, keys):
            stack = kj[pl.ds(first, number), pair * 2 + half, 0:keys, :].reshape(number * keys, 128)
            s = matmul(stack, q, NT)
            m = peak[half]
            tops, terms = [], []
            for i in range(number):
                part = s[i * keys:(i + 1) * keys]
                t = jnp.max(part, axis=0, keepdims=True)
                w = jnp.exp2((part - t) * EXP2_SCALE).astype(jnp.bfloat16)
                terms.append(matmul(vj[first + i, pair * 2 + half, :, 0:keys], w))
                tops.append(t)
            top = functools.reduce(jnp.maximum, tops, m)
            new = acc[half] * jnp.exp2((m - top) * EXP2_SCALE)
            for t, x in zip(tops, terms):
                new = new + x * jnp.exp2((t - top) * EXP2_SCALE)
            acc[half] = new
            peak[half] = top

        def units(first, many, number, keys):
            def go(i, _):
                unit(first + i * number, number, keys)
                return 0

            lax.fori_loop(0, many, go, 0)

        for i, keys in enumerate(SIZES):
            many = count[i]
            units(starts(i), many // 2, 2, keys)
            units(starts(i) + many - many % 2, many % 2, 1, keys)

    low = lax.broadcasted_iota(jnp.int32, (1, 128), 1) < 64

    def emit(i, _):
        lanes = pl.ds(pl.multiple_of(i * 128, 128), 128)
        a, b = acc[0, 0:136, lanes], acc[1, 0:136, lanes]
        pa, pb = peak[0, :, lanes], peak[1, :, lanes]
        for odd in range(2):
            if odd:
                whole = jnp.where(low, pltpu.roll(a, 64, 1), b)
                top = jnp.where(low, pltpu.roll(jnp.broadcast_to(pa, (8, 128)), 64, 1)[0:1], pb)
            else:
                whole = jnp.where(low, a, pltpu.roll(b, 64, 1))
                top = jnp.where(low, pa, pltpu.roll(jnp.broadcast_to(pb, (8, 128)), 64, 1)[0:1])
            values, scale = encode(whole[0:128])
            o_ref[i * 2 + odd, 0] = values
            side_ref[i * 2 + odd, pl.ds(pair * 4, 4), :] = jnp.concatenate([top, whole[128:129], scale, scale], axis=0)
        return 0

    lax.fori_loop(0, 32, emit, 0, unroll=8)


def encode(x):
    largest = jnp.maximum(jnp.max(jnp.abs(x), axis=0, keepdims=True), 1e-30)
    whole = jnp.round(x * (TOP16 / largest)).astype(jnp.int32).astype(jnp.int16)
    return whole, largest * (1.0 / TOP16)


def attend(lists, plan, gathered, pool_k, pool_v, suffix_k, suffix_v):
    hbm = pl.BlockSpec(memory_space=pl.ANY)
    return pl.pallas_call(
        attend_kernel,
        grid=(2,),
        in_specs=[
            pl.BlockSpec(memory_space=pltpu.SMEM),
            pl.BlockSpec(memory_space=pltpu.SMEM),
            pl.BlockSpec((64, 128, 128), lambda i: (0, i, 0)),
            hbm, hbm,
            pl.BlockSpec((32, 128), lambda i: (0, 0)),
            pl.BlockSpec((32, 128), lambda i: (0, 0)),
        ],
        out_specs=[pl.BlockSpec((64, 1, 128, 128), lambda i: (0, i, 0, 0)), pl.BlockSpec((64, 8, 128), lambda i: (0, 0, 0))],
        out_shape=[jax.ShapeDtypeStruct((64, 2, 128, 128), jnp.int16), jax.ShapeDtypeStruct((64, 8, 128), jnp.float32)],
        scratch_shapes=[
            pltpu.VMEM((2 * JOBS, 4, 256, 128), jnp.bfloat16), pltpu.VMEM((2 * JOBS, 4, 144, 256), jnp.bfloat16),
            pltpu.VMEM((4, 16, 128), jnp.bfloat16), pltpu.VMEM((4, 144, 128), jnp.bfloat16), pltpu.VMEM((2, 32, 128), jnp.float32),
            pltpu.VMEM((2, 1, 4096), jnp.float32), pltpu.VMEM((2, 144, 4096), jnp.float32),
            pltpu.SMEM((2, 2 * JOBS), jnp.int32), pltpu.SMEM((3,), jnp.int32), pltpu.SemaphoreType.DMA((2, 2 * JOBS)),
        ],
        compiler_params=pltpu.CompilerParams(vmem_limit_bytes=62 * 2**20),
        name="attend",
    )(lists, plan, gathered, pool_k, pool_v, suffix_k, suffix_v)


def merge(parts):
    top = functools.reduce(jnp.maximum, [side[0:1] for _, side in parts])
    total, weighted = 0.0, 0.0
    for values, side in parts:
        factor = jnp.exp2((side[0:1] - top) * EXP2_SCALE)
        total = total + side[1:2] * factor
        weighted = weighted + values.astype(jnp.int32).astype(jnp.float32) * (side[2:3] * factor)
    return weighted, top, total


def merge_kernel(o_ref, side_ref, out_ref, *scratch):
    buffers = [scratch[i * 12:(i + 1) * 12] for i in range(3)]
    rows, swapped, wide, send_sem, recv_sem, own_sem, swap_sem = scratch[36:]
    place, core = position()

    def cut(part, at):
        pair, pairs, row, many = SPLIT[part]
        where = [slice(None)] * 3
        where[part] = at
        return (o_ref.at[where[0], where[1], where[2], pl.ds(pair, pairs), pl.ds(row, many)],
                side_ref.at[where[0], where[1], where[2]])

    def line(part, ref, at, other=slice(None)):
        return ref.at[other, at] if part == 1 else ref.at[at, other]

    def copies(part, stage, step):
        p0, p0s, r1, r1s, m1, m1s, r2, r2s, m2, m2s, r3, r3s = buffers[part]
        axis = (part + stage) % 3
        to = along(place, axis, step)
        if stage == 0:
            sources, targets = cut(part, to[axis]), (r1, r1s)
        elif stage == 1:
            sources, targets = (line(part, m1, to[axis]), line(part, m1s, to[axis])), (r2, r2s)
        else:
            sources, targets = (m2.at[to[axis]], m2s.at[to[axis]]), (r3, r3s)
        return [
            pltpu.make_async_remote_copy(
                source, target.at[step - 1], send_sem.at[part, stage, step - 1, i], recv_sem.at[part, stage, step - 1, i],
                device_id=device(to, core), device_id_type=MESH)
            for i, (source, target) in enumerate(zip(sources, targets))
        ]

    def start(part, stage):
        for step in (2, 1, 3):
            for copy in copies(part, stage, step):
                copy.start()

    def arrive(part, stage):
        for step in (1, 2, 3):
            for copy in copies(part, stage, step):
                copy.wait_recv()

    def combine(part, sources):
        pair, pairs = SPLIT[part][:2]
        return [merge([(values[i], side[(pair + i) * 4:(pair + i) * 4 + 4]) for values, side in sources]) for i in range(pairs)]

    def fold(part, sources, target, target_side):
        pair = SPLIT[part][0]
        sides = [jnp.zeros((4, 128), jnp.float32)] * 2
        for i, (weighted, top, total) in enumerate(combine(part, sources)):
            values, scale = encode(weighted)
            target[i] = values
            sides[pair + i] = jnp.concatenate([top, total, scale, scale], axis=0)
        target_side[...] = jnp.concatenate(sides, axis=0)

    keep = [[pltpu.make_async_copy(source, target, own_sem.at[part, i])
             for i, (source, target) in enumerate(zip(cut(part, place[part]), buffers[part][:2]))] for part in range(3)]
    for pair in keep:
        for copy in pair:
            copy.start()
    greet(place, core)
    for part in range(3):
        start(part, 0)
    for part in range(3):
        p0, p0s, r1, r1s, m1, m1s = buffers[part][:6]
        for copy in keep[part]:
            copy.wait()
        arrive(part, 0)

        def first(n, _):
            i, j = n // 4, n % 4
            fold(part, [(p0.at[i, j], p0s.at[i, j])] + [(r1.at[k, i, j], r1s.at[k, i, j]) for k in range(3)],
                 m1.at[i, j], m1s.at[i, j])
            return 0

        lax.fori_loop(0, 16, first, 0)
        start(part, 1)
    for part in range(3):
        m1, m1s, r2, r2s, m2, m2s = buffers[part][4:10]
        at = place[(part + 1) % 3]
        arrive(part, 1)

        def second(c, _):
            fold(part, [(line(part, m1, at, c), line(part, m1s, at, c))] + [(r2.at[k, c], r2s.at[k, c]) for k in range(3)],
                 m2.at[c], m2s.at[c])
            return 0

        lax.fori_loop(0, 4, second, 0)
        start(part, 2)
    pieces = [[], []]
    for part in range(3):
        m2, m2s, r3, r3s = buffers[part][8:]
        at = place[(part + 2) % 3]
        arrive(part, 2)
        sources = [(m2.at[at], m2s.at[at])] + [(r3.at[k], r3s.at[k]) for k in range(3)]
        for i, (weighted, _, total) in enumerate(combine(part, sources)):
            pieces[SPLIT[part][0] + i].append(weighted / total)
    for pair in range(2):
        done = jnp.transpose(jnp.concatenate(pieces[pair], axis=0))
        for g in range(2):
            for owner in range(2):
                rows[owner, pair * 2 + g] = done[g * 64 + owner * 32:g * 64 + (owner + 1) * 32]
    swap = pltpu.make_async_remote_copy(rows.at[1 - core], swapped, swap_sem.at[0], swap_sem.at[1],
                                        device_id=device(place, 1 - core), device_id_type=MESH)
    swap.start()

    def tokens(grouped):
        split = grouped.reshape(4, 4, 8, 128)
        return jnp.stack([jnp.concatenate([split[g, t] for g in range(4)], axis=0) for t in range(4)])

    wide[:, pl.ds(pl.multiple_of(core * 32, 32), 32), :] = tokens(rows[core])
    swap.wait()
    wide[:, pl.ds(pl.multiple_of((1 - core) * 32, 32), 32), :] = tokens(swapped[...])
    out_ref[...] = wide[...].astype(jnp.bfloat16)

    for part in range(3):
        for stage in range(3):
            for step in (1, 2, 3):
                for copy in copies(part, stage, step):
                    copy.wait_send()


def merge_parts(values, side):
    hbm, vmem = pl.BlockSpec(memory_space=pl.ANY), pl.BlockSpec(memory_space=pltpu.VMEM)
    dma = pltpu.SemaphoreType.DMA
    buffers = []
    for _, pairs, _, many in SPLIT:
        for lead in ((4, 4), (3, 4, 4), (4, 4), (3, 4), (4,), (3,)):
            buffers += [pltpu.VMEM((*lead, pairs, many, 128), jnp.int16), pltpu.VMEM((*lead, 8, 128), jnp.float32)]
    return pl.pallas_call(
        merge_kernel,
        out_shape=jax.ShapeDtypeStruct((4, 64, 128), jnp.bfloat16),
        in_specs=[hbm, hbm],
        out_specs=vmem,
        scratch_shapes=[
            *buffers,
            pltpu.VMEM((2, 4, 32, 128), jnp.float32), pltpu.VMEM((4, 32, 128), jnp.float32), pltpu.VMEM((4, 64, 128), jnp.float32),
            dma((3, 3, 3, 2)), dma((3, 3, 3, 2)), dma((3, 2)), dma((2,)),
        ],
        compiler_params=pltpu.CompilerParams(collective_id=1, has_side_effects=True, vmem_limit_bytes=62 * 2**20),
        name="merge_parts",
    )(values.reshape(4, 4, 4, 2, 128, 128), side.reshape(4, 4, 4, 8, 128))


def local(queries, suffix_k, suffix_v, pool_k, pool_v, list_holder, list_slot, list_valid):
    pool_k, pool_v = pool_k.reshape(16, 1024, 128), pool_v.reshape(16, 1024, 128)
    gathered, lists, keys, values, plan = gather_queries(queries, list_holder.reshape(8), list_slot, list_valid, pool_k, pool_v)
    near = suffix_k.reshape(32, 128), suffix_v.reshape(32, 128)
    parts, side = attend(lists, plan, gathered.reshape(64, 256, 128), keys, values, *near)
    return merge_parts(parts, side)


def solution(mesh):
    in_specs = (
        P(("store", "ctx", "head"), None, None),
        P(("store", "ctx"), "head", None),
        P(("store", "ctx"), "head", None),
        P(("store", "ctx"), None, "head", None),
        P(("store", "ctx"), None, "head", None),
        P(("store", "ctx"), None),
        P(("store", "ctx")),
        P(("store", "ctx")),
    )
    out_specs = P(("store", "ctx", "head"), None, None)
    return jax.shard_map(local, mesh=mesh, in_specs=in_specs, out_specs=out_specs, check_vma=False)
```

```python
import functools
import math

import jax
import jax.numpy as jnp
from jax import lax
from jax.experimental import pallas as pl
from jax.experimental.pallas import tpu as pltpu
from jax.sharding import PartitionSpec as P

NEG = -1e30
EXP2_SCALE = math.log2(math.e) / math.sqrt(128)
NT = (((1,), (1,)), ((), ()))
NN = (((1,), (0,)), ((), ()))
MESH = pl.DeviceIdType.MESH
PARTS = ((0, 48, 48), (96, 32, 32), (160, 48, 48))
SPLIT = ((0, 1, 0, 80), (1, 1, 0, 80), (0, 2, 80, 48))
ORDERS = ((0, 1, 2), (1, 2, 0), (0, 2, 1))
JOBS = 14
COSTS = (115, 90, 72)
SIZES = (256, 192, 128)
TOP16 = 32767.0


def matmul(a, b, dims=NN):
    return lax.dot_general(a, b, dims, preferred_element_type=jnp.float32)


def position():
    ctx = lax.axis_index("ctx")
    return [lax.axis_index("store"), ctx // 4, ctx % 4], lax.axis_index("head")


def device(place, core):
    return (place[0], place[1] * 4 + place[2], core)


def along(place, axis, step):
    moved = list(place)
    moved[axis] = (place[axis] + step) % 4
    return moved


def greet(place, core):
    barrier = pltpu.get_barrier_semaphore()
    for axis in range(3):
        for step in (1, 2, 3):
            pl.semaphore_signal(barrier, 1, device_id=device(along(place, axis, step), core), device_id_type=MESH)
    pl.semaphore_signal(barrier, 1, device_id=device(place, 1 - core), device_id_type=MESH)
    pl.semaphore_wait(barrier, 10)


def size_class(valid):
    return jnp.where(valid > SIZES[1], 0, jnp.where(valid > SIZES[2], 1, 2))


def pick(options, index):
    value = options[0]
    for i in range(1, len(options)):
        value = jnp.where(index == i, options[i], value)
    return value


def whole(reduce, x):
    return reduce(reduce(x, axis=1, keepdims=True), axis=0, keepdims=True)


def plan_moves(holder, valid, number):
    live = (valid > 0) & (number >= 0)
    size = size_class(valid)
    cost = jnp.where(live, pick([jnp.full_like(valid, c) for c in COSTS], size), 0)
    loads = [whole(jnp.sum, jnp.where(holder == s, cost, 0)) for s in range(4)]
    none = jnp.full((1, 1), -1, jnp.int32)
    moves = [[none, none] for _ in range(4)]
    for _ in range(5):
        most = functools.reduce(jnp.maximum, loads)
        giver = jnp.where(loads[0] == most, 0, jnp.where(loads[1] == most, 1, jnp.where(loads[2] == most, 2, 3)))
        ways = []
        for way, step in enumerate((1, 3)):
            free = pick([moves[s][way] for s in range(4)], giver) < 0
            ways.append(jnp.where(free, pick(loads[step:] + loads[:step], giver), 1 << 20))
        way = jnp.where(ways[0] <= ways[1], 0, 1)
        least = jnp.minimum(ways[0], ways[1])
        gone = [pick([moves[s][w] for s in range(4)], giver) for w in range(2)]
        at = live & (holder == giver) & (number != gone[0]) & (number != gone[1])
        found = [whole(jnp.max, jnp.where(at & (size == k), number, -1)) for k in range(3)]
        entry, saved = none, jnp.zeros((1, 1), jnp.int32)
        for k in (2, 1, 0):
            helps = (found[k] >= 0) & (least + COSTS[k] < most)
            entry, saved = jnp.where(helps, found[k], entry), jnp.where(helps, COSTS[k], saved)
        for s in range(4):
            takes = ((giver == (s + 3) % 4) & (way == 0)) | ((giver == (s + 1) % 4) & (way == 1))
            loads[s] = loads[s] - jnp.where(giver == s, saved, 0) + jnp.where(takes, saved, 0)
            for w in range(2):
                moves[s][w] = jnp.where((giver == s) & (way == w) & (entry >= 0), entry, moves[s][w])
    return moves


def gather_kernel(q_ref, holder_ref, slot_ref, valid_ref, pk_ref, pv_ref, all_ref, lists_ref, kp_ref, vp_ref, plan_ref,
                  list_ref, table, plan_tile, out_k, out_v, in_k, in_v, theirs, send, own, raw_k, raw_v, keys, values, wide_k, wide_v,
                  swap_sem, list_sem, own_sem, send_sem, recv_sem, raw_sem, out_sem, plan_sem, move_send, move_recv):
    place, core = position()

    def raw_copies(n):
        return [pltpu.make_async_copy(pk_ref.at[n], raw_k.at[n], raw_sem.at[0, n]),
                pltpu.make_async_copy(pv_ref.at[n], raw_v.at[n], raw_sem.at[1, n])]

    def out_copies(n):
        return [pltpu.make_async_copy(keys.at[n], kp_ref.at[n], out_sem.at[0, n]),
                pltpu.make_async_copy(values.at[n], vp_ref.at[n], out_sem.at[1, n])]

    def over(first, last, function):
        def go(n, _):
            function(n)
            return 0
        lax.fori_loop(first, last, go, 0)

    def begin(n):
        for copy in raw_copies(n):
            copy.start()

    over(0, 16, begin)
    row = lax.broadcasted_iota(jnp.int32, (8, 128), 0)
    lane = lax.broadcasted_iota(jnp.int32, (8, 128), 1)
    tile = jnp.zeros((8, 128), jnp.int32)
    for e in range(8):
        for r, ref in enumerate((holder_ref, slot_ref, valid_ref)):
            tile = jnp.where((row == r) & (lane == e), ref[e], tile)
    list_ref[...] = tile
    greet(place, core)
    swap = pltpu.make_async_remote_copy(
        q_ref.at[:, pl.ds((1 - core) * 32, 32), :], theirs, swap_sem.at[0], swap_sem.at[1],
        device_id=device(place, 1 - core), device_id_type=MESH)
    swap.start()
    lists = []
    for step in (1, 2, 3):
        copy = pltpu.make_async_remote_copy(
            list_ref, table.at[place[0]], list_sem.at[0, step - 1], list_sem.at[1, step - 1],
            device_id=device(along(place, 0, step), core), device_id_type=MESH)
        copy.start()
        lists.append(copy)
    own_lists = pltpu.make_async_copy(list_ref, table.at[place[0]], own_sem.at[1])
    own_lists.start()

    def grouped(tokens):
        wide = tokens.astype(jnp.float32).reshape(4, 4, 8, 128)
        return jnp.stack([wide[:, g].reshape(32, 128) for g in range(4)]).astype(jnp.bfloat16)

    def regroup(n, of_k=raw_k, of_v=raw_v, first=0):
        wide_k[...] = of_k[n - first].astype(jnp.float32)
        wide_v[...] = of_v[n - first].astype(jnp.float32)
        for g in range(4):
            keys[n, g] = wide_k[pl.ds(g, 256, stride=4), :].astype(jnp.bfloat16)
            values[n, g] = jnp.transpose(wide_v[pl.ds(g, 256, stride=4), :]).astype(jnp.bfloat16)
        for copy in out_copies(n):
            copy.start()

    send[:, pl.ds(core * 32, 32), :] = grouped(q_ref[:, pl.ds(core * 32, 32), :])
    swap.wait()
    send[:, pl.ds((1 - core) * 32, 32), :] = grouped(theirs[...])
    own[...] = send[...].reshape(256, 128)
    keep = pltpu.make_async_copy(own, all_ref.at[place[0], place[1], place[2]], own_sem.at[0])
    keep.start()

    def links(part, phase, which):
        order = ORDERS[part]
        axis, (at, upper, lower) = order[phase], PARTS[part]
        halves = pl.ds(at, upper), pl.ds(at + upper, lower)
        plan = ((0, 1, 0), (1, 3, 0), (1, 1, 0), (0, 3, 0), (0, 1, 3), (1, 3, 1))
        copies = []
        for i in which:
            half, step, origin = plan[i]
            source = along(place, axis, origin)
            where = [slice(None) if d in order[:phase] else source[d] for d in range(3)]
            block = all_ref.at[where[0], where[1], where[2], halves[half]]
            copies.append(pltpu.make_async_remote_copy(
                own.at[halves[half]] if phase == 0 and origin == 0 else block, block,
                send_sem.at[part, phase, i], recv_sem.at[part, phase, i],
                device_id=device(along(place, axis, step), core), device_id_type=MESH))
        return copies

    def move(way):
        to = device(along(place, 0, (1, 3)[way]), core)
        return [
            pltpu.make_async_remote_copy(source.at[way], target.at[way], move_send.at[way, i], move_recv.at[way, i],
                                         device_id=to, device_id_type=MESH)
            for i, (source, target) in enumerate(((out_k, in_k), (out_v, in_v)))
        ]

    def ready(n):
        for copy in raw_copies(n):
            copy.wait()

    def balance():
        for copy in lists:
            copy.wait()
        own_lists.wait()
        pltpu.make_async_copy(table, lists_ref, plan_sem.at[0]).start()
        over(0, 16, ready)
        holder, slots, valid = (table[:, i, :] for i in range(3))
        lanes = lax.broadcasted_iota(jnp.int32, (4, 128), 1)
        number = jnp.where(lanes < 8, lax.broadcasted_iota(jnp.int32, (4, 128), 0) * 8 + lanes, -1)
        moves = plan_moves(holder, valid, number)
        given = [pick([moves[s][way] for s in range(4)], place[0]) for way in range(2)]
        taken = [pick([moves[s][way] for s in range(4)], (place[0] + (3, 1)[way]) % 4) for way in range(2)]
        for way in range(2):
            slot = jnp.max(jnp.where((number == given[way]) & (number >= 0), slots, 0))
            out_k[way] = raw_k[slot]
            out_v[way] = raw_v[slot]
            for copy in move(way):
                copy.start()
        first_row = row == 0
        told = jnp.zeros((8, 128), jnp.int32)
        for i, value in enumerate(given + taken):
            told = jnp.where(first_row & (lane == i), value, told)
        plan_tile[...] = told
        pltpu.make_async_copy(plan_tile, plan_ref, plan_sem.at[1]).start()

    for phase in range(3):
        for part in range(3):
            if phase:
                for i in (2, 3, 4, 5):
                    links(part, phase - 1, (i,))[0].wait_recv()
            if phase == 1 and part == 0:
                keep.wait()
            for copy in links(part, phase, range(4)):
                copy.start()
        over(*((0, 0), (2, 4), (6, 10))[phase], regroup)
        for part in range(3):
            for i in (0, 1):
                links(part, phase, (i,))[0].wait_recv()
                links(part, phase, (i + 4,))[0].start()
        if phase == 0:
            balance()
        over(*((0, 2), (4, 6), (10, 16))[phase], regroup)
    for way in range(2):
        for copy in move(way):
            copy.wait()
    over(16, 18, functools.partial(regroup, of_k=in_k, of_v=in_v, first=16))
    for part in range(3):
        for i in (2, 3, 4, 5):
            links(part, 2, (i,))[0].wait_recv()
    for part in range(3):
        for phase in range(3):
            for copy in links(part, phase, range(6)):
                copy.wait_send()
    pltpu.make_async_copy(plan_tile, plan_ref, plan_sem.at[1]).wait()
    pltpu.make_async_copy(table, lists_ref, plan_sem.at[0]).wait()

    def finish(n):
        for copy in out_copies(n):
            copy.wait()

    over(0, 18, finish)


def gather_queries(queries, holder, slot, valid, pool_k, pool_v):
    hbm = pl.BlockSpec(memory_space=pl.ANY)
    vmem, smem = pl.BlockSpec(memory_space=pltpu.VMEM), pl.BlockSpec(memory_space=pltpu.SMEM)
    dma = pltpu.SemaphoreType.DMA
    return pl.pallas_call(
        gather_kernel,
        out_shape=[
            jax.ShapeDtypeStruct((4, 4, 4, 256, 128), jnp.bfloat16), jax.ShapeDtypeStruct((4, 8, 128), jnp.int32),
            jax.ShapeDtypeStruct((18, 4, 256, 128), jnp.bfloat16), jax.ShapeDtypeStruct((18, 4, 128, 256), jnp.bfloat16),
            jax.ShapeDtypeStruct((8, 128), jnp.int32),
        ],
        in_specs=[vmem, smem, smem, smem, hbm, hbm],
        out_specs=[hbm] * 5,
        scratch_shapes=[
            pltpu.VMEM((8, 128), jnp.int32), pltpu.VMEM((4, 8, 128), jnp.int32), pltpu.VMEM((8, 128), jnp.int32),
            *[pltpu.VMEM((2, 1024, 128), jnp.bfloat16)] * 4, pltpu.VMEM((4, 32, 128), jnp.bfloat16),
            pltpu.VMEM((4, 64, 128), jnp.bfloat16), pltpu.VMEM((256, 128), jnp.bfloat16),
            pltpu.VMEM((16, 1024, 128), jnp.bfloat16), pltpu.VMEM((16, 1024, 128), jnp.bfloat16),
            pltpu.VMEM((18, 4, 256, 128), jnp.bfloat16), pltpu.VMEM((18, 4, 128, 256), jnp.bfloat16),
            pltpu.VMEM((1024, 128), jnp.float32), pltpu.VMEM((1024, 128), jnp.float32),
            dma((2,)), dma((2, 3)), dma((2,)), dma((3, 3, 6)), dma((3, 3, 6)), dma((2, 16)), dma((2, 18)), dma((2,)), dma((2, 2)), dma((2, 2)),
        ],
        compiler_params=pltpu.CompilerParams(collective_id=0, has_side_effects=True, vmem_limit_bytes=62 * 2**20),
        name="gather_queries",
    )(queries, holder, slot, valid, pool_k, pool_v)


def attend_kernel(list_ref, plan_ref, q_ref, pk_ref, pv_ref, near_k_ref, near_v_ref, o_ref, side_ref,
                  kj, vj, sk_ref, sv_ref, near, peak, acc, jobs, count, sem):
    def starts(size):
        return (0, JOBS, JOBS - count[2])[size]

    @pl.when(pl.program_id(0) == 0)
    def prepare():
        store = lax.axis_index("store")
        for i in range(len(SIZES)):
            count[i] = 0

        def add(slot, valid):
            size = size_class(valid)
            n = jnp.where(size == 0, count[0], jnp.where(size == 1, JOBS + count[1], JOBS - 1 - count[2]))
            jobs[0, n] = slot
            jobs[1, n] = valid
            count[size] = count[size] + 1
            pltpu.make_async_copy(pk_ref.at[slot], kj.at[n], sem.at[0, n]).start()
            pltpu.make_async_copy(pv_ref.at[slot], vj.at[n, :, 0:128], sem.at[1, n]).start()

        def look(i, _):
            r, e = i // 8, i % 8
            kept = (i != plan_ref[0, 0]) & (i != plan_ref[0, 1])

            @pl.when((list_ref[r, 0, e] == store) & (list_ref[r, 2, e] > 0) & kept)
            def _():
                add(list_ref[r, 1, e], list_ref[r, 2, e])
            return 0

        for way in range(2):
            entry = plan_ref[0, 2 + way]

            @pl.when(entry >= 0)
            def _():
                add(16 + way, list_ref[entry // 8, 2, entry % 8])

        lax.fori_loop(0, 32, look, 0)
        near[0] = near_k_ref[...].astype(jnp.float32)
        near[1] = near_v_ref[...].astype(jnp.float32)
        ones = jnp.where(lax.broadcasted_iota(jnp.int32, (16, 128), 1) < 8, 1.0, 0.0)
        for g in range(4):
            k, v = near[0, pl.ds(g, 8, stride=4), :], near[1, pl.ds(g, 8, stride=4), :]
            sk_ref[g] = jnp.concatenate([k, jnp.zeros((8, 128), jnp.float32)], axis=0).astype(jnp.bfloat16)
            v = jnp.transpose(jnp.concatenate([v, jnp.zeros((120, 128), jnp.float32)], axis=0))
            sv_ref[g] = jnp.concatenate([v, ones], axis=0).astype(jnp.bfloat16)

        def fix(n, _):
            slot, valid = jobs[0, n], jobs[1, n]
            pltpu.make_async_copy(pk_ref.at[slot], kj.at[n], sem.at[0, n]).wait()
            pltpu.make_async_copy(pv_ref.at[slot], vj.at[n, :, 0:128], sem.at[1, n]).wait()
            live_row = lax.broadcasted_iota(jnp.int32, (256, 128), 0) < valid
            live_lane = lax.broadcasted_iota(jnp.int32, (128, 256), 1) < valid
            for g in range(4):
                keys = kj[n, g].astype(jnp.float32)
                kj[n, g] = jnp.where(live_row, keys, keys[0:1]).astype(jnp.bfloat16)
                vj[n, g, 0:128] = jnp.where(live_lane, vj[n, g, 0:128].astype(jnp.float32), 0.0).astype(jnp.bfloat16)
                vj[n, g, 128:144] = live_lane[0:16].astype(jnp.float32).astype(jnp.bfloat16)
            return 0

        for i in range(3):
            lax.fori_loop(starts(i), starts(i) + count[i], fix, 0)

    pair = pl.program_id(0)
    suffix_at = (lax.axis_index("store") * 16 + lax.axis_index("ctx")) * 8
    key_at = suffix_at + lax.broadcasted_iota(jnp.int32, (8, 4096), 0)
    query_at = lax.broadcasted_iota(jnp.int32, (8, 4096), 1) // 8
    live = key_at <= query_at
    for half in range(2):
        q = q_ref[:, half * 64:(half + 1) * 64, :].reshape(4096, 128)
        s = matmul(sk_ref[pair * 2 + half], q, NT)[0:8]
        s = jnp.where(live, s, NEG)
        t = jnp.max(s, axis=0, keepdims=True)
        w = jnp.where(live, jnp.exp2((s - t) * EXP2_SCALE), 0.0)
        w = jnp.concatenate([w, jnp.zeros((120, 4096), jnp.float32)], axis=0).astype(jnp.bfloat16)
        acc[half] = matmul(sv_ref[pair * 2 + half], w)
        peak[half] = t

        def unit(first, number, keys):
            stack = kj[pl.ds(first, number), pair * 2 + half, 0:keys, :].reshape(number * keys, 128)
            s = matmul(stack, q, NT)
            m = peak[half]
            tops, terms = [], []
            for i in range(number):
                part = s[i * keys:(i + 1) * keys]
                t = jnp.max(part, axis=0, keepdims=True)
                w = jnp.exp2((part - t) * EXP2_SCALE).astype(jnp.bfloat16)
                terms.append(matmul(vj[first + i, pair * 2 + half, :, 0:keys], w))
                tops.append(t)
            top = functools.reduce(jnp.maximum, tops, m)
            new = acc[half] * jnp.exp2((m - top) * EXP2_SCALE)
            for t, x in zip(tops, terms):
                new = new + x * jnp.exp2((t - top) * EXP2_SCALE)
            acc[half] = new
            peak[half] = top

        def units(first, many, number, keys):
            def go(i, _):
                unit(first + i * number, number, keys)
                return 0

            lax.fori_loop(0, many, go, 0)

        for i, keys in enumerate(SIZES):
            many = count[i]
            units(starts(i), many // 2, 2, keys)
            units(starts(i) + many - many % 2, many % 2, 1, keys)

    low = lax.broadcasted_iota(jnp.int32, (1, 128), 1) < 64

    def emit(i, _):
        lanes = pl.ds(pl.multiple_of(i * 128, 128), 128)
        a, b = acc[0, 0:136, lanes], acc[1, 0:136, lanes]
        pa, pb = peak[0, :, lanes], peak[1, :, lanes]
        for odd in range(2):
            if odd:
                whole = jnp.where(low, pltpu.roll(a, 64, 1), b)
                top = jnp.where(low, pltpu.roll(jnp.broadcast_to(pa, (8, 128)), 64, 1)[0:1], pb)
            else:
                whole = jnp.where(low, a, pltpu.roll(b, 64, 1))
                top = jnp.where(low, pa, pltpu.roll(jnp.broadcast_to(pb, (8, 128)), 64, 1)[0:1])
            values, scale = encode(whole[0:128])
            o_ref[i * 2 + odd, 0] = values
            side_ref[i * 2 + odd, pl.ds(pair * 4, 4), :] = jnp.concatenate([top, whole[128:129], scale, scale], axis=0)
        return 0

    lax.fori_loop(0, 32, emit, 0, unroll=8)


def encode(x):
    largest = jnp.maximum(jnp.max(jnp.abs(x), axis=0, keepdims=True), 1e-30)
    whole = jnp.round(x * (TOP16 / largest)).astype(jnp.int32).astype(jnp.int16)
    return whole, largest * (1.0 / TOP16)


def attend(lists, plan, gathered, pool_k, pool_v, suffix_k, suffix_v):
    hbm = pl.BlockSpec(memory_space=pl.ANY)
    return pl.pallas_call(
        attend_kernel,
        grid=(2,),
        in_specs=[
            pl.BlockSpec(memory_space=pltpu.SMEM),
            pl.BlockSpec(memory_space=pltpu.SMEM),
            pl.BlockSpec((64, 128, 128), lambda i: (0, i, 0)),
            hbm, hbm,
            pl.BlockSpec((32, 128), lambda i: (0, 0)),
            pl.BlockSpec((32, 128), lambda i: (0, 0)),
        ],
        out_specs=[pl.BlockSpec((64, 1, 128, 128), lambda i: (0, i, 0, 0)), pl.BlockSpec((64, 8, 128), lambda i: (0, 0, 0))],
        out_shape=[jax.ShapeDtypeStruct((64, 2, 128, 128), jnp.int16), jax.ShapeDtypeStruct((64, 8, 128), jnp.float32)],
        scratch_shapes=[
            pltpu.VMEM((2 * JOBS, 4, 256, 128), jnp.bfloat16), pltpu.VMEM((2 * JOBS, 4, 144, 256), jnp.bfloat16),
            pltpu.VMEM((4, 16, 128), jnp.bfloat16), pltpu.VMEM((4, 144, 128), jnp.bfloat16), pltpu.VMEM((2, 32, 128), jnp.float32),
            pltpu.VMEM((2, 1, 4096), jnp.float32), pltpu.VMEM((2, 144, 4096), jnp.float32),
            pltpu.SMEM((2, 2 * JOBS), jnp.int32), pltpu.SMEM((3,), jnp.int32), pltpu.SemaphoreType.DMA((2, 2 * JOBS)),
        ],
        compiler_params=pltpu.CompilerParams(vmem_limit_bytes=62 * 2**20),
        name="attend",
    )(lists, plan, gathered, pool_k, pool_v, suffix_k, suffix_v)


def merge(parts):
    top = functools.reduce(jnp.maximum, [side[0:1] for _, side in parts])
    total, weighted = 0.0, 0.0
    for values, side in parts:
        factor = jnp.exp2((side[0:1] - top) * EXP2_SCALE)
        total = total + side[1:2] * factor
        weighted = weighted + values.astype(jnp.int32).astype(jnp.float32) * (side[2:3] * factor)
    return weighted, top, total


def merge_kernel(o_ref, side_ref, out_ref, *scratch):
    buffers = [scratch[i * 18:(i + 1) * 18] for i in range(3)]
    rows, swapped, wide, send_sem, recv_sem, ring_send, ring_recv, own_sem, swap_sem = scratch[54:]
    place, core = position()

    def cut(part, at, half=None):
        pair, pairs, row, many = SPLIT[part]
        where = [slice(None)] * 3
        where[part] = at
        if half is not None:
            where[1 if part == 0 else 0] = pl.ds(half * 2, 2)
        return (o_ref.at[where[0], where[1], where[2], pl.ds(pair, pairs), pl.ds(row, many)],
                side_ref.at[where[0], where[1], where[2]])

    def line(part, ref, at, other=slice(None)):
        return ref.at[other, at] if part == 1 else ref.at[at, other]

    def ring(part, way, kind):
        r1, r1s, _, _, rin, rins, rout, routs = buffers[part][2:10]
        step = (1, 3)[way]
        to = along(place, part, step)
        if kind == 0:
            sources, targets = cut(part, along(place, part, 2)[part], way), (rin.at[way], rins.at[way])
        else:
            half = 1 - way if kind == 1 else way
            sources = cut(part, to[part], half) if kind == 1 else (rout.at[way], routs.at[way])
            targets = r1.at[way, pl.ds(half * 2, 2)], r1s.at[way, pl.ds(half * 2, 2)]
        return [
            pltpu.make_async_remote_copy(
                source, target, ring_send.at[part, way, kind, i], ring_recv.at[part, way, kind, i],
                device_id=device(to, core), device_id_type=MESH)
            for i, (source, target) in enumerate(zip(sources, targets))
        ]

    def copies(part, stage, step):
        m1, m1s, r2, r2s, m2, m2s, r3, r3s = buffers[part][10:]
        axis = (part + stage) % 3
        to = along(place, axis, step)
        if stage == 1:
            sources, targets = (line(part, m1, to[axis]), line(part, m1s, to[axis])), (r2, r2s)
        else:
            sources, targets = (m2.at[to[axis]], m2s.at[to[axis]]), (r3, r3s)
        return [
            pltpu.make_async_remote_copy(
                source, target.at[step - 1], send_sem.at[part, stage - 1, step - 1, i], recv_sem.at[part, stage - 1, step - 1, i],
                device_id=device(to, core), device_id_type=MESH)
            for i, (source, target) in enumerate(zip(sources, targets))
        ]

    def start(part, stage):
        for step in (2, 1, 3):
            for copy in copies(part, stage, step):
                copy.start()

    def arrive(part, stage):
        for step in (1, 2, 3):
            for copy in copies(part, stage, step):
                copy.wait_recv()

    def combine(part, sources):
        pair, pairs = SPLIT[part][:2]
        return [merge([(values[i], side[(pair + i) * 4:(pair + i) * 4 + 4]) for values, side in sources]) for i in range(pairs)]

    def fold(part, sources, target, target_side):
        pair = SPLIT[part][0]
        sides = [jnp.zeros((4, 128), jnp.float32)] * 2
        for i, (weighted, top, total) in enumerate(combine(part, sources)):
            values, scale = encode(weighted)
            target[i] = values
            sides[pair + i] = jnp.concatenate([top, total, scale, scale], axis=0)
        target_side[...] = jnp.concatenate(sides, axis=0)

    def keep(part):
        p0, p0s, _, _, near, nears = buffers[part][:6]
        moves = list(zip(cut(part, place[part]), (p0, p0s)))
        for way in range(2):
            moves += zip(cut(part, along(place, part, (1, 3)[way])[part], way), (near.at[way], nears.at[way]))
        return [pltpu.make_async_copy(source, target, own_sem.at[part, i]) for i, (source, target) in enumerate(moves)]

    for part in range(3):
        for copy in keep(part):
            copy.start()
    greet(place, core)
    for kind in range(2):
        for part in range(3):
            for way in range(2):
                for copy in ring(part, way, kind):
                    copy.start()
    for part in range(3):
        near, nears, rin, rins, rout, routs = buffers[part][4:10]
        for copy in keep(part):
            copy.wait()
        for way in range(2):
            for copy in ring(part, way, 0):
                copy.wait_recv()

            def passing(n, _):
                i, j = n // 4, n % 4
                fold(part, [(near.at[way, i, j], nears.at[way, i, j]), (rin.at[way, i, j], rins.at[way, i, j])],
                     rout.at[way, i, j], routs.at[way, i, j])
                return 0

            lax.fori_loop(0, 8, passing, 0, unroll=4)
            for copy in ring(part, way, 2):
                copy.start()
    for part in range(3):
        p0, p0s, r1, r1s = buffers[part][:4]
        m1, m1s = buffers[part][10:12]
        for way in range(2):
            for kind in (1, 2):
                for copy in ring(part, way, kind):
                    copy.wait_recv()

        def first(n, _):
            i, j = n // 4, n % 4
            fold(part, [(p0.at[i, j], p0s.at[i, j])] + [(r1.at[k, i, j], r1s.at[k, i, j]) for k in range(2)],
                 m1.at[i, j], m1s.at[i, j])
            return 0

        lax.fori_loop(0, 16, first, 0, unroll=4)
        start(part, 1)
    for part in range(3):
        m1, m1s, r2, r2s, m2, m2s = buffers[part][10:16]
        at = place[(part + 1) % 3]
        arrive(part, 1)

        def second(c, _):
            fold(part, [(line(part, m1, at, c), line(part, m1s, at, c))] + [(r2.at[k, c], r2s.at[k, c]) for k in range(3)],
                 m2.at[c], m2s.at[c])
            return 0

        lax.fori_loop(0, 4, second, 0, unroll=4)
        start(part, 2)
    pieces = [[], []]
    for part in range(3):
        m2, m2s, r3, r3s = buffers[part][14:]
        at = place[(part + 2) % 3]
        arrive(part, 2)
        sources = [(m2.at[at], m2s.at[at])] + [(r3.at[k], r3s.at[k]) for k in range(3)]
        for i, (weighted, _, total) in enumerate(combine(part, sources)):
            pieces[SPLIT[part][0] + i].append(weighted / total)
    for pair in range(2):
        done = jnp.transpose(jnp.concatenate(pieces[pair], axis=0))
        for g in range(2):
            for owner in range(2):
                rows[owner, pair * 2 + g] = done[g * 64 + owner * 32:g * 64 + (owner + 1) * 32]
    swap = pltpu.make_async_remote_copy(rows.at[1 - core], swapped, swap_sem.at[0], swap_sem.at[1],
                                        device_id=device(place, 1 - core), device_id_type=MESH)
    swap.start()

    def tokens(grouped):
        split = grouped.reshape(4, 4, 8, 128)
        return jnp.stack([jnp.concatenate([split[g, t] for g in range(4)], axis=0) for t in range(4)])

    wide[:, pl.ds(pl.multiple_of(core * 32, 32), 32), :] = tokens(rows[core])
    swap.wait()
    wide[:, pl.ds(pl.multiple_of((1 - core) * 32, 32), 32), :] = tokens(swapped[...])
    out_ref[...] = wide[...].astype(jnp.bfloat16)

    for part in range(3):
        for way in range(2):
            for kind in range(3):
                for copy in ring(part, way, kind):
                    copy.wait_send()
        for stage in (1, 2):
            for step in (1, 2, 3):
                for copy in copies(part, stage, step):
                    copy.wait_send()


def merge_parts(values, side):
    hbm, vmem = pl.BlockSpec(memory_space=pl.ANY), pl.BlockSpec(memory_space=pltpu.VMEM)
    dma = pltpu.SemaphoreType.DMA
    buffers = []
    for _, pairs, _, many in SPLIT:
        for lead in ((4, 4), (2, 4, 4), (2, 2, 4), (2, 2, 4), (2, 2, 4), (4, 4), (3, 4), (4,), (3,)):
            buffers += [pltpu.VMEM((*lead, pairs, many, 128), jnp.int16), pltpu.VMEM((*lead, 8, 128), jnp.float32)]
    return pl.pallas_call(
        merge_kernel,
        out_shape=jax.ShapeDtypeStruct((4, 64, 128), jnp.bfloat16),
        in_specs=[hbm, hbm],
        out_specs=vmem,
        scratch_shapes=[
            *buffers,
            pltpu.VMEM((2, 4, 32, 128), jnp.float32), pltpu.VMEM((4, 32, 128), jnp.float32), pltpu.VMEM((4, 64, 128), jnp.float32),
            dma((3, 2, 3, 2)), dma((3, 2, 3, 2)), dma((3, 2, 3, 2)), dma((3, 2, 3, 2)), dma((3, 6)), dma((2,)),
        ],
        compiler_params=pltpu.CompilerParams(collective_id=1, has_side_effects=True, vmem_limit_bytes=62 * 2**20),
        name="merge_parts",
    )(values.reshape(4, 4, 4, 2, 128, 128), side.reshape(4, 4, 4, 8, 128))


def local(queries, suffix_k, suffix_v, pool_k, pool_v, list_holder, list_slot, list_valid):
    pool_k, pool_v = pool_k.reshape(16, 1024, 128), pool_v.reshape(16, 1024, 128)
    gathered, lists, keys, values, plan = gather_queries(queries, list_holder.reshape(8), list_slot, list_valid, pool_k, pool_v)
    near = suffix_k.reshape(32, 128), suffix_v.reshape(32, 128)
    parts, side = attend(lists, plan, gathered.reshape(64, 256, 128), keys, values, *near)
    return merge_parts(parts, side)


def solution(mesh):
    in_specs = (
        P(("store", "ctx", "head"), None, None),
        P(("store", "ctx"), "head", None),
        P(("store", "ctx"), "head", None),
        P(("store", "ctx"), None, "head", None),
        P(("store", "ctx"), None, "head", None),
        P(("store", "ctx"), None),
        P(("store", "ctx")),
        P(("store", "ctx")),
    )
    out_specs = P(("store", "ctx", "head"), None, None)
    return jax.shard_map(local, mesh=mesh, in_specs=in_specs, out_specs=out_specs, check_vma=False)
```

```python
import functools
import math

import jax
import jax.numpy as jnp
from jax import lax
from jax.experimental import pallas as pl
from jax.experimental.pallas import tpu as pltpu
from jax.sharding import PartitionSpec as P

NEG = -1e30
EXP2_SCALE = math.log2(math.e) / math.sqrt(128)
NT = (((1,), (1,)), ((), ()))
NN = (((1,), (0,)), ((), ()))
MESH = pl.DeviceIdType.MESH
PARTS = ((0, 48, 48), (96, 32, 32), (160, 48, 48))
SPLIT = ((0, 1, 0, 96), (1, 1, 0, 96), (0, 2, 96, 32))
ORDERS = ((0, 1, 2), (1, 2, 0), (0, 2, 1))
JOBS = 14
COSTS = (115, 90, 72)
SIZES = (256, 192, 128)
TOP16 = 32767.0


def matmul(a, b, dims=NN):
    return lax.dot_general(a, b, dims, preferred_element_type=jnp.float32)


def position():
    ctx = lax.axis_index("ctx")
    return [lax.axis_index("store"), ctx // 4, ctx % 4], lax.axis_index("head")


def device(place, core):
    return (place[0], place[1] * 4 + place[2], core)


def along(place, axis, step):
    moved = list(place)
    moved[axis] = (place[axis] + step) % 4
    return moved


def greet(place, core):
    barrier = pltpu.get_barrier_semaphore()
    for axis in range(3):
        for step in (1, 2, 3):
            pl.semaphore_signal(barrier, 1, device_id=device(along(place, axis, step), core), device_id_type=MESH)
    pl.semaphore_signal(barrier, 1, device_id=device(place, 1 - core), device_id_type=MESH)
    pl.semaphore_wait(barrier, 10)


def size_class(valid):
    return jnp.where(valid > SIZES[1], 0, jnp.where(valid > SIZES[2], 1, 2))


def pick(options, index):
    value = options[0]
    for i in range(1, len(options)):
        value = jnp.where(index == i, options[i], value)
    return value


def whole(reduce, x):
    return reduce(reduce(x, axis=1, keepdims=True), axis=0, keepdims=True)


def plan_moves(holder, valid, number):
    live = (valid > 0) & (number >= 0)
    size = size_class(valid)
    cost = jnp.where(live, pick([jnp.full_like(valid, c) for c in COSTS], size), 0)
    loads = [whole(jnp.sum, jnp.where(holder == s, cost, 0)) for s in range(4)]
    none = jnp.full((1, 1), -1, jnp.int32)
    moves = [[none, none] for _ in range(4)]
    for _ in range(5):
        most = functools.reduce(jnp.maximum, loads)
        giver = jnp.where(loads[0] == most, 0, jnp.where(loads[1] == most, 1, jnp.where(loads[2] == most, 2, 3)))
        ways = []
        for way, step in enumerate((1, 3)):
            free = pick([moves[s][way] for s in range(4)], giver) < 0
            ways.append(jnp.where(free, pick(loads[step:] + loads[:step], giver), 1 << 20))
        way = jnp.where(ways[0] <= ways[1], 0, 1)
        least = jnp.minimum(ways[0], ways[1])
        gone = [pick([moves[s][w] for s in range(4)], giver) for w in range(2)]
        at = live & (holder == giver) & (number != gone[0]) & (number != gone[1])
        found = [whole(jnp.max, jnp.where(at & (size == k), number, -1)) for k in range(3)]
        entry, saved = none, jnp.zeros((1, 1), jnp.int32)
        for k in (2, 1, 0):
            helps = (found[k] >= 0) & (least + COSTS[k] < most)
            entry, saved = jnp.where(helps, found[k], entry), jnp.where(helps, COSTS[k], saved)
        for s in range(4):
            takes = ((giver == (s + 3) % 4) & (way == 0)) | ((giver == (s + 1) % 4) & (way == 1))
            loads[s] = loads[s] - jnp.where(giver == s, saved, 0) + jnp.where(takes, saved, 0)
            for w in range(2):
                moves[s][w] = jnp.where((giver == s) & (way == w) & (entry >= 0), entry, moves[s][w])
    return moves


def gather_kernel(q_ref, holder_ref, slot_ref, valid_ref, pk_ref, pv_ref, all_ref, lists_ref, kp_ref, vp_ref, plan_ref,
                  list_ref, table, plan_tile, out_k, out_v, in_k, in_v, theirs, send, own, raw_k, raw_v, keys, values, wide_k, wide_v,
                  swap_sem, list_sem, own_sem, send_sem, recv_sem, raw_sem, out_sem, plan_sem, move_send, move_recv):
    place, core = position()

    def raw_copies(n):
        return [pltpu.make_async_copy(pk_ref.at[n], raw_k.at[n], raw_sem.at[0, n]),
                pltpu.make_async_copy(pv_ref.at[n], raw_v.at[n], raw_sem.at[1, n])]

    def out_copies(n):
        return [pltpu.make_async_copy(keys.at[n], kp_ref.at[n], out_sem.at[0, n]),
                pltpu.make_async_copy(values.at[n], vp_ref.at[n], out_sem.at[1, n])]

    def over(first, last, function):
        def go(n, _):
            function(n)
            return 0
        lax.fori_loop(first, last, go, 0)

    def begin(n):
        for copy in raw_copies(n):
            copy.start()

    over(0, 16, begin)
    row = lax.broadcasted_iota(jnp.int32, (8, 128), 0)
    lane = lax.broadcasted_iota(jnp.int32, (8, 128), 1)
    tile = jnp.zeros((8, 128), jnp.int32)
    for e in range(8):
        for r, ref in enumerate((holder_ref, slot_ref, valid_ref)):
            tile = jnp.where((row == r) & (lane == e), ref[e], tile)
    list_ref[...] = tile
    greet(place, core)
    swap = pltpu.make_async_remote_copy(
        q_ref.at[:, pl.ds((1 - core) * 32, 32), :], theirs, swap_sem.at[0], swap_sem.at[1],
        device_id=device(place, 1 - core), device_id_type=MESH)
    swap.start()
    lists = []
    for step in (1, 2, 3):
        copy = pltpu.make_async_remote_copy(
            list_ref, table.at[place[0]], list_sem.at[0, step - 1], list_sem.at[1, step - 1],
            device_id=device(along(place, 0, step), core), device_id_type=MESH)
        copy.start()
        lists.append(copy)
    own_lists = pltpu.make_async_copy(list_ref, table.at[place[0]], own_sem.at[1])
    own_lists.start()

    def grouped(tokens):
        wide = tokens.astype(jnp.float32).reshape(4, 4, 8, 128)
        return jnp.stack([wide[:, g].reshape(32, 128) for g in range(4)]).astype(jnp.bfloat16)

    def regroup(n, of_k=raw_k, of_v=raw_v, first=0):
        wide_k[...] = of_k[n - first].astype(jnp.float32)
        wide_v[...] = of_v[n - first].astype(jnp.float32)
        for g in range(4):
            keys[n, g] = wide_k[pl.ds(g, 256, stride=4), :].astype(jnp.bfloat16)
            values[n, g] = jnp.transpose(wide_v[pl.ds(g, 256, stride=4), :]).astype(jnp.bfloat16)
        for copy in out_copies(n):
            copy.start()

    send[:, pl.ds(core * 32, 32), :] = grouped(q_ref[:, pl.ds(core * 32, 32), :])
    swap.wait()
    send[:, pl.ds((1 - core) * 32, 32), :] = grouped(theirs[...])
    own[...] = send[...].reshape(256, 128)
    keep = pltpu.make_async_copy(own, all_ref.at[place[0], place[1], place[2]], own_sem.at[0])
    keep.start()

    def links(part, phase, which):
        order = ORDERS[part]
        axis, (at, upper, lower) = order[phase], PARTS[part]
        halves = pl.ds(at, upper), pl.ds(at + upper, lower)
        plan = ((0, 1, 0), (1, 3, 0), (1, 1, 0), (0, 3, 0), (0, 1, 3), (1, 3, 1))
        copies = []
        for i in which:
            half, step, origin = plan[i]
            if phase == 0 and i > 3:
                step, origin = 2, 0
            source = along(place, axis, origin)
            where = [slice(None) if d in order[:phase] else source[d] for d in range(3)]
            block = all_ref.at[where[0], where[1], where[2], halves[half]]
            copies.append(pltpu.make_async_remote_copy(
                own.at[halves[half]] if phase == 0 and origin == 0 else block, block,
                send_sem.at[part, phase, i], recv_sem.at[part, phase, i],
                device_id=device(along(place, axis, step), core), device_id_type=MESH))
        return copies

    def move(way):
        to = device(along(place, 0, (1, 3)[way]), core)
        return [
            pltpu.make_async_remote_copy(source.at[way], target.at[way], move_send.at[way, i], move_recv.at[way, i],
                                         device_id=to, device_id_type=MESH)
            for i, (source, target) in enumerate(((out_k, in_k), (out_v, in_v)))
        ]

    def ready(n):
        for copy in raw_copies(n):
            copy.wait()

    def balance():
        for copy in lists:
            copy.wait()
        own_lists.wait()
        pltpu.make_async_copy(table, lists_ref, plan_sem.at[0]).start()
        over(0, 16, ready)
        holder, slots, valid = (table[:, i, :] for i in range(3))
        lanes = lax.broadcasted_iota(jnp.int32, (4, 128), 1)
        number = jnp.where(lanes < 8, lax.broadcasted_iota(jnp.int32, (4, 128), 0) * 8 + lanes, -1)
        moves = plan_moves(holder, valid, number)
        given = [pick([moves[s][way] for s in range(4)], place[0]) for way in range(2)]
        taken = [pick([moves[s][way] for s in range(4)], (place[0] + (3, 1)[way]) % 4) for way in range(2)]
        for way in range(2):
            slot = jnp.max(jnp.where((number == given[way]) & (number >= 0), slots, 0))
            out_k[way] = raw_k[slot]
            out_v[way] = raw_v[slot]
            for copy in move(way):
                copy.start()
        first_row = row == 0
        told = jnp.zeros((8, 128), jnp.int32)
        for i, value in enumerate(given + taken):
            told = jnp.where(first_row & (lane == i), value, told)
        plan_tile[...] = told
        pltpu.make_async_copy(plan_tile, plan_ref, plan_sem.at[1]).start()

    for phase in range(3):
        for part in range(3):
            if phase:
                for i in (2, 3, 4, 5):
                    links(part, phase - 1, (i,))[0].wait_recv()
            if phase == 1 and part == 0:
                keep.wait()
            for copy in links(part, phase, range(4 if phase else 6)):
                copy.start()
        over(*((0, 0), (2, 4), (6, 10))[phase], regroup)
        for part in range(3):
            for i in (0, 1):
                links(part, phase, (i,))[0].wait_recv()
                if phase:
                    links(part, phase, (i + 4,))[0].start()
        if phase == 0:
            balance()
        over(*((0, 2), (4, 6), (10, 16))[phase], regroup)
    for way in range(2):
        for copy in move(way):
            copy.wait()
    over(16, 18, functools.partial(regroup, of_k=in_k, of_v=in_v, first=16))
    for part in range(3):
        for i in (2, 3, 4, 5):
            links(part, 2, (i,))[0].wait_recv()
    for part in range(3):
        for phase in range(3):
            for copy in links(part, phase, range(6)):
                copy.wait_send()
    pltpu.make_async_copy(plan_tile, plan_ref, plan_sem.at[1]).wait()
    pltpu.make_async_copy(table, lists_ref, plan_sem.at[0]).wait()

    def finish(n):
        for copy in out_copies(n):
            copy.wait()

    over(0, 18, finish)


def gather_queries(queries, holder, slot, valid, pool_k, pool_v):
    hbm = pl.BlockSpec(memory_space=pl.ANY)
    vmem, smem = pl.BlockSpec(memory_space=pltpu.VMEM), pl.BlockSpec(memory_space=pltpu.SMEM)
    dma = pltpu.SemaphoreType.DMA
    return pl.pallas_call(
        gather_kernel,
        out_shape=[
            jax.ShapeDtypeStruct((4, 4, 4, 256, 128), jnp.bfloat16), jax.ShapeDtypeStruct((4, 8, 128), jnp.int32),
            jax.ShapeDtypeStruct((18, 4, 256, 128), jnp.bfloat16), jax.ShapeDtypeStruct((18, 4, 128, 256), jnp.bfloat16),
            jax.ShapeDtypeStruct((8, 128), jnp.int32),
        ],
        in_specs=[vmem, smem, smem, smem, hbm, hbm],
        out_specs=[hbm] * 5,
        scratch_shapes=[
            pltpu.VMEM((8, 128), jnp.int32), pltpu.VMEM((4, 8, 128), jnp.int32), pltpu.VMEM((8, 128), jnp.int32),
            *[pltpu.VMEM((2, 1024, 128), jnp.bfloat16)] * 4, pltpu.VMEM((4, 32, 128), jnp.bfloat16),
            pltpu.VMEM((4, 64, 128), jnp.bfloat16), pltpu.VMEM((256, 128), jnp.bfloat16),
            pltpu.VMEM((16, 1024, 128), jnp.bfloat16), pltpu.VMEM((16, 1024, 128), jnp.bfloat16),
            pltpu.VMEM((18, 4, 256, 128), jnp.bfloat16), pltpu.VMEM((18, 4, 128, 256), jnp.bfloat16),
            pltpu.VMEM((1024, 128), jnp.float32), pltpu.VMEM((1024, 128), jnp.float32),
            dma((2,)), dma((2, 3)), dma((2,)), dma((3, 3, 6)), dma((3, 3, 6)), dma((2, 16)), dma((2, 18)), dma((2,)), dma((2, 2)), dma((2, 2)),
        ],
        compiler_params=pltpu.CompilerParams(collective_id=0, has_side_effects=True, vmem_limit_bytes=62 * 2**20),
        name="gather_queries",
    )(queries, holder, slot, valid, pool_k, pool_v)


def attend_kernel(list_ref, plan_ref, q_ref, pk_ref, pv_ref, near_k_ref, near_v_ref, o_ref, side_ref,
                  kj, vj, sk_ref, sv_ref, near, peak, acc, jobs, count, sem):
    def starts(size):
        return (0, JOBS, JOBS - count[2])[size]

    @pl.when(pl.program_id(0) == 0)
    def prepare():
        store = lax.axis_index("store")
        for i in range(len(SIZES)):
            count[i] = 0

        def add(slot, valid):
            size = size_class(valid)
            n = jnp.where(size == 0, count[0], jnp.where(size == 1, JOBS + count[1], JOBS - 1 - count[2]))
            jobs[0, n] = slot
            jobs[1, n] = valid
            count[size] = count[size] + 1
            pltpu.make_async_copy(pk_ref.at[slot], kj.at[n], sem.at[0, n]).start()
            pltpu.make_async_copy(pv_ref.at[slot], vj.at[n, :, 0:128], sem.at[1, n]).start()

        def look(i, _):
            r, e = i // 8, i % 8
            kept = (i != plan_ref[0, 0]) & (i != plan_ref[0, 1])

            @pl.when((list_ref[r, 0, e] == store) & (list_ref[r, 2, e] > 0) & kept)
            def _():
                add(list_ref[r, 1, e], list_ref[r, 2, e])
            return 0

        for way in range(2):
            entry = plan_ref[0, 2 + way]

            @pl.when(entry >= 0)
            def _():
                add(16 + way, list_ref[entry // 8, 2, entry % 8])

        lax.fori_loop(0, 32, look, 0)
        near[0] = near_k_ref[...].astype(jnp.float32)
        near[1] = near_v_ref[...].astype(jnp.float32)
        ones = jnp.where(lax.broadcasted_iota(jnp.int32, (16, 128), 1) < 8, 1.0, 0.0)
        for g in range(4):
            k, v = near[0, pl.ds(g, 8, stride=4), :], near[1, pl.ds(g, 8, stride=4), :]
            sk_ref[g] = jnp.concatenate([k, jnp.zeros((8, 128), jnp.float32)], axis=0).astype(jnp.bfloat16)
            v = jnp.transpose(jnp.concatenate([v, jnp.zeros((120, 128), jnp.float32)], axis=0))
            sv_ref[g] = jnp.concatenate([v, ones], axis=0).astype(jnp.bfloat16)

    def fix(n, _):
        slot, valid = jobs[0, n], jobs[1, n]
        pltpu.make_async_copy(pk_ref.at[slot], kj.at[n], sem.at[0, n]).wait()
        pltpu.make_async_copy(pv_ref.at[slot], vj.at[n, :, 0:128], sem.at[1, n]).wait()
        live_row = lax.broadcasted_iota(jnp.int32, (256, 128), 0) < valid
        live_lane = lax.broadcasted_iota(jnp.int32, (128, 256), 1) < valid
        for g in range(4):
            vj[n, g, 128:144] = live_lane[0:16].astype(jnp.float32).astype(jnp.bfloat16)

        @pl.when(valid < 256)
        def _():
            for g in range(4):
                keys = kj[n, g].astype(jnp.float32)
                kj[n, g] = jnp.where(live_row, keys, keys[0:1]).astype(jnp.bfloat16)
                vj[n, g, 0:128] = jnp.where(live_lane, vj[n, g, 0:128].astype(jnp.float32), 0.0).astype(jnp.bfloat16)
        return 0

    pair = pl.program_id(0)
    suffix_at = (lax.axis_index("store") * 16 + lax.axis_index("ctx")) * 8
    key_at = suffix_at + lax.broadcasted_iota(jnp.int32, (8, 4096), 0)
    query_at = lax.broadcasted_iota(jnp.int32, (8, 4096), 1) // 8
    live = key_at <= query_at
    for half in range(2):
        q = q_ref[:, half * 64:(half + 1) * 64, :].reshape(4096, 128)
        s = matmul(sk_ref[pair * 2 + half], q, NT)[0:8]
        s = jnp.where(live, s, NEG)
        t = jnp.max(s, axis=0, keepdims=True)
        w = jnp.where(live, jnp.exp2((s - t) * EXP2_SCALE), 0.0)
        w = jnp.concatenate([w, jnp.zeros((120, 4096), jnp.float32)], axis=0).astype(jnp.bfloat16)
        acc[half] = matmul(sv_ref[pair * 2 + half], w)
        peak[half] = t

        if half == 0:
            @pl.when(pair == 0)
            def _():
                for i in range(3):
                    lax.fori_loop(starts(i), starts(i) + count[i], fix, 0)

        def unit(first, number, keys):
            stack = kj[pl.ds(first, number), pair * 2 + half, 0:keys, :].reshape(number * keys, 128)
            s = matmul(stack, q, NT)
            m = peak[half]
            tops, terms = [], []
            for i in range(number):
                part = s[i * keys:(i + 1) * keys]
                t = jnp.max(part, axis=0, keepdims=True)
                w = jnp.exp2((part - t) * EXP2_SCALE).astype(jnp.bfloat16)
                terms.append(matmul(vj[first + i, pair * 2 + half, :, 0:keys], w))
                tops.append(t)
            top = functools.reduce(jnp.maximum, tops, m)
            new = acc[half] * jnp.exp2((m - top) * EXP2_SCALE)
            for t, x in zip(tops, terms):
                new = new + x * jnp.exp2((t - top) * EXP2_SCALE)
            acc[half] = new
            peak[half] = top

        def units(first, many, number, keys):
            def go(i, _):
                unit(first + i * number, number, keys)
                return 0

            lax.fori_loop(0, many, go, 0)

        for i, keys in enumerate(SIZES):
            many = count[i]
            units(starts(i), many // 2, 2, keys)
            units(starts(i) + many - many % 2, many % 2, 1, keys)

    low = lax.broadcasted_iota(jnp.int32, (1, 128), 1) < 64

    def emit(i, _):
        lanes = pl.ds(pl.multiple_of(i * 128, 128), 128)
        a, b = acc[0, 0:136, lanes], acc[1, 0:136, lanes]
        pa, pb = peak[0, :, lanes], peak[1, :, lanes]
        for odd in range(2):
            if odd:
                whole = jnp.where(low, pltpu.roll(a, 64, 1), b)
                top = jnp.where(low, pltpu.roll(jnp.broadcast_to(pa, (8, 128)), 64, 1)[0:1], pb)
            else:
                whole = jnp.where(low, a, pltpu.roll(b, 64, 1))
                top = jnp.where(low, pa, pltpu.roll(jnp.broadcast_to(pb, (8, 128)), 64, 1)[0:1])
            values, scale = encode(whole[0:128])
            o_ref[i * 2 + odd, 0] = values
            side_ref[i * 2 + odd, 0] = jnp.concatenate([top, whole[128:129], scale, scale], axis=0)
        return 0

    lax.fori_loop(0, 32, emit, 0, unroll=16)


def encode(x):
    largest = jnp.maximum(jnp.max(jnp.abs(x), axis=0, keepdims=True), 1e-30)
    whole = jnp.round(x * (TOP16 / largest)).astype(jnp.int32).astype(jnp.int16)
    return whole, largest * (1.0 / TOP16)


def attend(lists, plan, gathered, pool_k, pool_v, suffix_k, suffix_v):
    hbm = pl.BlockSpec(memory_space=pl.ANY)
    return pl.pallas_call(
        attend_kernel,
        grid=(2,),
        in_specs=[
            pl.BlockSpec(memory_space=pltpu.SMEM),
            pl.BlockSpec(memory_space=pltpu.SMEM),
            pl.BlockSpec((64, 128, 128), lambda i: (0, i, 0)),
            hbm, hbm,
            pl.BlockSpec((32, 128), lambda i: (0, 0)),
            pl.BlockSpec((32, 128), lambda i: (0, 0)),
        ],
        out_specs=[pl.BlockSpec((64, 1, 128, 128), lambda i: (0, i, 0, 0)), pl.BlockSpec((64, 1, 4, 128), lambda i: (0, i, 0, 0))],
        out_shape=[jax.ShapeDtypeStruct((64, 2, 128, 128), jnp.int16), jax.ShapeDtypeStruct((64, 2, 4, 128), jnp.float32)],
        scratch_shapes=[
            pltpu.VMEM((2 * JOBS, 4, 256, 128), jnp.bfloat16), pltpu.VMEM((2 * JOBS, 4, 144, 256), jnp.bfloat16),
            pltpu.VMEM((4, 16, 128), jnp.bfloat16), pltpu.VMEM((4, 144, 128), jnp.bfloat16), pltpu.VMEM((2, 32, 128), jnp.float32),
            pltpu.VMEM((2, 1, 4096), jnp.float32), pltpu.VMEM((2, 144, 4096), jnp.float32),
            pltpu.SMEM((2, 2 * JOBS), jnp.int32), pltpu.SMEM((3,), jnp.int32), pltpu.SemaphoreType.DMA((2, 2 * JOBS)),
        ],
        compiler_params=pltpu.CompilerParams(vmem_limit_bytes=62 * 2**20),
        name="attend",
    )(lists, plan, gathered, pool_k, pool_v, suffix_k, suffix_v)


def merge(parts):
    top = functools.reduce(jnp.maximum, [side[0:1] for _, side in parts])
    total, weighted = 0.0, 0.0
    for values, side in parts:
        factor = jnp.exp2((side[0:1] - top) * EXP2_SCALE)
        total = total + side[1:2] * factor
        weighted = weighted + values.astype(jnp.int32).astype(jnp.float32) * (side[2:3] * factor)
    return weighted, top, total


def merge_kernel(o_ref, side_ref, out_ref, *scratch):
    buffers = [scratch[i * 18:(i + 1) * 18] for i in range(3)]
    rows, swapped, wide, send_sem, recv_sem, ring_send, ring_recv, own_sem, swap_sem = scratch[54:]
    place, core = position()

    def cut(part, at, half=None):
        pair, pairs, row, many = SPLIT[part]
        where = [slice(None)] * 3
        where[part] = at
        if half is not None:
            where[1 if part == 0 else 0] = pl.ds(half * 2, 2)
        return (o_ref.at[where[0], where[1], where[2], pl.ds(pair, pairs), pl.ds(row, many)],
                side_ref.at[where[0], where[1], where[2], pl.ds(pair, pairs)])

    def line(part, ref, at, other=slice(None)):
        return ref.at[other, at] if part == 1 else ref.at[at, other]

    def ring(part, way, kind):
        r1, r1s, _, _, rin, rins, rout, routs = buffers[part][2:10]
        step = (1, 3)[way]
        to = along(place, part, step)
        if kind == 0:
            sources, targets = cut(part, along(place, part, 2)[part], way), (rin.at[way], rins.at[way])
        else:
            half = 1 - way if kind == 1 else way
            sources = cut(part, to[part], half) if kind == 1 else (rout.at[way], routs.at[way])
            targets = r1.at[way, pl.ds(half * 2, 2)], r1s.at[way, pl.ds(half * 2, 2)]
        return [
            pltpu.make_async_remote_copy(
                source, target, ring_send.at[part, way, kind, i], ring_recv.at[part, way, kind, i],
                device_id=device(to, core), device_id_type=MESH)
            for i, (source, target) in enumerate(zip(sources, targets))
        ]

    def copies(part, stage, step):
        m1, m1s, r2, r2s, m2, m2s, r3, r3s = buffers[part][10:]
        axis = (part + stage) % 3
        to = along(place, axis, step)
        if stage == 1:
            sources, targets = (line(part, m1, to[axis]), line(part, m1s, to[axis])), (r2, r2s)
        else:
            sources, targets = (m2.at[to[axis]], m2s.at[to[axis]]), (r3, r3s)
        return [
            pltpu.make_async_remote_copy(
                source, target.at[step - 1], send_sem.at[part, stage - 1, step - 1, i], recv_sem.at[part, stage - 1, step - 1, i],
                device_id=device(to, core), device_id_type=MESH)
            for i, (source, target) in enumerate(zip(sources, targets))
        ]

    def start(part, stage):
        for step in (2, 1, 3):
            for copy in copies(part, stage, step):
                copy.start()

    def arrive(part, stage):
        for step in (1, 2, 3):
            for copy in copies(part, stage, step):
                copy.wait_recv()

    def combine(part, sources):
        return [merge([(values[i], side[i]) for values, side in sources]) for i in range(SPLIT[part][1])]

    def fold(part, sources, target, target_side):
        for i, (weighted, top, total) in enumerate(combine(part, sources)):
            values, scale = encode(weighted)
            target[i] = values
            target_side[i] = jnp.concatenate([top, total, scale, scale], axis=0)

    def keep(part):
        p0, p0s, _, _, near, nears = buffers[part][:6]
        moves = list(zip(cut(part, place[part]), (p0, p0s)))
        for way in range(2):
            moves += zip(cut(part, along(place, part, (1, 3)[way])[part], way), (near.at[way], nears.at[way]))
        return [pltpu.make_async_copy(source, target, own_sem.at[part, i]) for i, (source, target) in enumerate(moves)]

    for part in range(3):
        for copy in keep(part):
            copy.start()
    greet(place, core)
    for kind in range(2):
        for part in range(3):
            for way in range(2):
                for copy in ring(part, way, kind):
                    copy.start()
    for part in range(3):
        near, nears, rin, rins, rout, routs = buffers[part][4:10]
        for copy in keep(part):
            copy.wait()
        for way in range(2):
            for copy in ring(part, way, 0):
                copy.wait_recv()

            def passing(n, _):
                i, j = n // 4, n % 4
                fold(part, [(near.at[way, i, j], nears.at[way, i, j]), (rin.at[way, i, j], rins.at[way, i, j])],
                     rout.at[way, i, j], routs.at[way, i, j])
                return 0

            lax.fori_loop(0, 8, passing, 0, unroll=4)
            for copy in ring(part, way, 2):
                copy.start()
    for part in range(3):
        p0, p0s, r1, r1s = buffers[part][:4]
        m1, m1s = buffers[part][10:12]
        for way in range(2):
            for kind in (1, 2):
                for copy in ring(part, way, kind):
                    copy.wait_recv()

        def first(n, _):
            i, j = n // 4, n % 4
            fold(part, [(p0.at[i, j], p0s.at[i, j])] + [(r1.at[k, i, j], r1s.at[k, i, j]) for k in range(2)],
                 m1.at[i, j], m1s.at[i, j])
            return 0

        lax.fori_loop(0, 16, first, 0, unroll=4)
        start(part, 1)
    for part in range(3):
        m1, m1s, r2, r2s, m2, m2s = buffers[part][10:16]
        at = place[(part + 1) % 3]
        arrive(part, 1)

        def second(c, _):
            fold(part, [(line(part, m1, at, c), line(part, m1s, at, c))] + [(r2.at[k, c], r2s.at[k, c]) for k in range(3)],
                 m2.at[c], m2s.at[c])
            return 0

        lax.fori_loop(0, 4, second, 0, unroll=4)
        start(part, 2)
    pieces = [[], []]
    for part in range(3):
        m2, m2s, r3, r3s = buffers[part][14:]
        at = place[(part + 2) % 3]
        arrive(part, 2)
        sources = [(m2.at[at], m2s.at[at])] + [(r3.at[k], r3s.at[k]) for k in range(3)]
        for i, (weighted, _, total) in enumerate(combine(part, sources)):
            pieces[SPLIT[part][0] + i].append(weighted / total)
    for pair in range(2):
        done = jnp.transpose(jnp.concatenate(pieces[pair], axis=0))
        for g in range(2):
            for owner in range(2):
                rows[owner, pair * 2 + g] = done[g * 64 + owner * 32:g * 64 + (owner + 1) * 32]
    swap = pltpu.make_async_remote_copy(rows.at[1 - core], swapped, swap_sem.at[0], swap_sem.at[1],
                                        device_id=device(place, 1 - core), device_id_type=MESH)
    swap.start()

    def tokens(grouped):
        split = grouped.reshape(4, 4, 8, 128)
        return jnp.stack([jnp.concatenate([split[g, t] for g in range(4)], axis=0) for t in range(4)])

    wide[:, pl.ds(pl.multiple_of(core * 32, 32), 32), :] = tokens(rows[core])
    swap.wait()
    wide[:, pl.ds(pl.multiple_of((1 - core) * 32, 32), 32), :] = tokens(swapped[...])
    out_ref[...] = wide[...].astype(jnp.bfloat16)

    for part in range(3):
        for way in range(2):
            for kind in range(3):
                for copy in ring(part, way, kind):
                    copy.wait_send()
        for stage in (1, 2):
            for step in (1, 2, 3):
                for copy in copies(part, stage, step):
                    copy.wait_send()


def merge_parts(values, side):
    hbm, vmem = pl.BlockSpec(memory_space=pl.ANY), pl.BlockSpec(memory_space=pltpu.VMEM)
    dma = pltpu.SemaphoreType.DMA
    buffers = []
    for _, pairs, _, many in SPLIT:
        for lead in ((4, 4), (2, 4, 4), (2, 2, 4), (2, 2, 4), (2, 2, 4), (4, 4), (3, 4), (4,), (3,)):
            buffers += [pltpu.VMEM((*lead, pairs, many, 128), jnp.int16), pltpu.VMEM((*lead, pairs, 4, 128), jnp.float32)]
    return pl.pallas_call(
        merge_kernel,
        out_shape=jax.ShapeDtypeStruct((4, 64, 128), jnp.bfloat16),
        in_specs=[hbm, hbm],
        out_specs=vmem,
        scratch_shapes=[
            *buffers,
            pltpu.VMEM((2, 4, 32, 128), jnp.float32), pltpu.VMEM((4, 32, 128), jnp.float32), pltpu.VMEM((4, 64, 128), jnp.float32),
            dma((3, 2, 3, 2)), dma((3, 2, 3, 2)), dma((3, 2, 3, 2)), dma((3, 2, 3, 2)), dma((3, 6)), dma((2,)),
        ],
        compiler_params=pltpu.CompilerParams(collective_id=1, has_side_effects=True, vmem_limit_bytes=62 * 2**20),
        name="merge_parts",
    )(values.reshape(4, 4, 4, 2, 128, 128), side.reshape(4, 4, 4, 2, 4, 128))


def local(queries, suffix_k, suffix_v, pool_k, pool_v, list_holder, list_slot, list_valid):
    pool_k, pool_v = pool_k.reshape(16, 1024, 128), pool_v.reshape(16, 1024, 128)
    gathered, lists, keys, values, plan = gather_queries(queries, list_holder.reshape(8), list_slot, list_valid, pool_k, pool_v)
    near = suffix_k.reshape(32, 128), suffix_v.reshape(32, 128)
    parts, side = attend(lists, plan, gathered.reshape(64, 256, 128), keys, values, *near)
    return merge_parts(parts, side)


def solution(mesh):
    in_specs = (
        P(("store", "ctx", "head"), None, None),
        P(("store", "ctx"), "head", None),
        P(("store", "ctx"), "head", None),
        P(("store", "ctx"), None, "head", None),
        P(("store", "ctx"), None, "head", None),
        P(("store", "ctx"), None),
        P(("store", "ctx")),
        P(("store", "ctx")),
    )
    out_specs = P(("store", "ctx", "head"), None, None)
    return jax.shard_map(local, mesh=mesh, in_specs=in_specs, out_specs=out_specs, check_vma=False)
```
